128 devices in a mesh: node: 4 (over x), local: 32 (over y, z, core).
Axes of the slice: x: 4, y: 4, z: 4, core: 2. Of those that a mesh axis runs over, the one named last changes fastest.
Arguments:
- tokens: bfloat16 [16384, 7168], P(('node', 'local')), may hold values from -6 to 6
- expert_ids: int32 [16384, 8], P(('node', 'local')), may hold values from 0 to 255, all different within a row; in each aligned block of 128 rows (0 to 127, 128 to 255, ...) at most 5 rows name the same one
- route_weights: float32 [16384, 8], P(('node', 'local')), may hold values from 0.1 to 1
- grad_out: bfloat16 [16384, 7168], P(('node', 'local')), may hold values from -1.5 to 1.5
- gate_weight: bfloat16 [7168, 16384], P(None, ('node', 'local')), may hold values from -0.0625 to 0.0625
- up_weight: bfloat16 [7168, 16384], P(None, ('node', 'local')), may hold values from -0.0625 to 0.0625
- down_weight: bfloat16 [16384, 7168], P(('node', 'local')), may hold values from -0.1875 to 0.1875
Outputs:
- mixed: bfloat16 [16384, 7168], P(('node', 'local'))
- grad_tokens: bfloat16 [16384, 7168], P(('node', 'local'))
- grad_weights: float32 [16384, 8], P(('node', 'local'))
- grad_gate: bfloat16 [7168, 16384], P(None, ('node', 'local'))
- grad_up: bfloat16 [7168, 16384], P(None, ('node', 'local'))
- grad_down: bfloat16 [16384, 7168], P(('node', 'local'))
The draws below stay inside these ranges and needn't reach their ends.
Inputs may be any that keep to these rules, and one draw needn't show every extreme that they name: `expert_ids`: A row names 8 different ids. In the 128 rows of one device no id is named by more than 5 rows, a bound that some block reaches.
All inputs are finite; a program needn't handle non-finite values. Where the reference program divides by a largest or mean magnitude, that divisor is 1e-20 or more.
Results may differ from the reference program's by a relative error of at most 0.012.
Values may be sent and summed in bfloat16 or wider, within the bound.
A program may use at most 192 MiB of HBM per device.

```python
import math
import jax
import jax.numpy as jnp
import numpy as np
from jax import lax

D = 7168
FF = 1024
ROUTED = 256
TOP = 8
SPLIT = 8
TOK_DEV = 128
CAP = 5
EXPERTS = 16
TOKENS = 16384
DEVICES = 128


def levels(own_key, dims, cuts, low, largest):
    gain = 1.0
    for dim, shards_of in cuts:
        draws = jax.random.uniform(jax.random.fold_in(jax.random.fold_in(own_key, 6), dim), (shards_of,), jnp.float32, low / len(cuts), largest / len(cuts))
        gain = gain * jnp.repeat(jnp.exp(draws), dims[dim] // shards_of).reshape((-1,) + (1,) * (len(dims) - 1 - dim))
    return gain


def shared_out(own_key, own, number, rows, number_of, top, bound, lean):
    ranking = jax.random.permutation(own_key, number_of)
    crowded, ordinary = shares(number_of, rows * top, bound, lean, True), shares(number_of, rows * top, bound, lean, False)
    places = jnp.arange(number_of)

    def named(tallies, turn):
        used = int((tallies > 0).sum())
        fixed = max(1, used // 4)
        moved = fixed + (places - fixed + turn * (used - fixed)) % max(1, number_of - fixed)
        return jnp.zeros((number_of,), jnp.int32).at[ranking[jnp.where(places < fixed, places, moved)]].set(jnp.asarray(tallies, jnp.int32))

    tallies = jnp.where(number % 4 == 0, named(crowded, number // 4), named(ordinary, number - number // 4 - 1))
    mixed = jax.random.permutation(jax.random.fold_in(own, 3), number_of)
    donor, taker = mixed[0:number_of // 2 * 2:2], mixed[1:number_of // 2 * 2:2]
    margin = jnp.minimum(tallies[donor] - 1, bound - tallies[taker]) // 2
    margin = jnp.where((donor == ranking[0]) | (taker == ranking[0]) | (tallies[taker] == 0), 0, jnp.maximum(margin, 0))
    moved = jax.random.randint(jax.random.fold_in(own, 4), (number_of // 2,), 0, 1 << 20) % (margin + 1)
    tallies = tallies.at[donor].add(-moved).at[taker].add(moved)
    items = jnp.searchsorted(jnp.cumsum(tallies), jnp.arange(rows * top), side="right").astype(jnp.int32)
    listing = items.reshape(top, rows).T
    listing = listing[jax.random.permutation(jax.random.fold_in(own, 1), rows)]
    turn = jax.random.randint(jax.random.fold_in(own, 2), (rows, 1), 0, top)
    return jnp.take_along_axis(listing, (jnp.arange(top)[None, :] + turn) % top, axis=1)


def shares(count, total, most, slope, full):
    loads = [(1 << 20) // math.isqrt(standing ** slope) + 1 for standing in range(1, count + 1)]
    largest = most if full else min(most, max(-(-total // count), total * loads[0] // sum(loads)))
    least = 1 if total - largest >= count - 1 else 0
    given, spare = [largest] + [least] * (count - 1), total - largest - least * (count - 1)
    while spare > 0:
        movable = [i for i in range(1, count) if given[i] < largest] or [i for i in range(1, count) if given[i] < most]
        pool, budget = sum([loads[i] for i in movable]), spare
        for i in movable:
            addition = min(most - given[i], max(1, budget * loads[i] // pool), spare)
            given[i] = given[i] + addition
            spare = spare - addition
    return np.array(given)


def noise(own_key, shape, scale, bound, cuts=(), held_as=jnp.bfloat16):
    entries = scale * jax.random.normal(own_key, shape, jnp.float32)
    if cuts:
        entries = entries * levels(own_key, shape, cuts, -0.22, 0.18)
    return jnp.clip(entries, -bound, bound).astype(held_as)


def setup_inputs(seed: int = 0) -> dict:
    key_list = jax.random.split(jax.random.key(seed), 8)
    tokens = noise(key_list[0], (TOKENS, D), 1.0, 6.0, ((0, 128),))
    expert_ids_keys = jax.random.split(jax.random.fold_in(key_list[1], 1), TOKENS // TOK_DEV)
    expert_ids_turns = jax.random.permutation(jax.random.fold_in(key_list[1], 3), TOKENS // TOK_DEV)
    expert_ids = jax.vmap(lambda own, number: shared_out(jax.random.fold_in(key_list[1], 2), own, number, TOK_DEV, ROUTED, TOP, CAP, 2))(expert_ids_keys, expert_ids_turns).reshape((TOKENS, TOP))
    route_weights = jnp.clip(0.1 + 0.9 * jax.random.uniform(key_list[2], (TOKENS, TOP), jnp.float32) ** levels(key_list[2], (TOKENS, TOP), ((0, 128),), -0.2, 0.2), 0.1, 1.0)
    grad_out = noise(key_list[3], (TOKENS, D), 0.25, 1.5, ((0, 128),))
    gate_weight = noise(key_list[4], (D, EXPERTS * FF), D ** -0.5, 0.0625, ((1, 128),))
    up_weight = noise(key_list[5], (D, EXPERTS * FF), D ** -0.5, 0.0625, ((1, 128),))
    down_weight = noise(key_list[6], (EXPERTS * FF, D), FF ** -0.5, 0.1875, ((0, 128),))
    return {"tokens": tokens, "expert_ids": expert_ids, "route_weights": route_weights, "grad_out": grad_out, "gate_weight": gate_weight, "up_weight": up_weight, "down_weight": down_weight}


def reference(tokens, expert_ids, route_weights, grad_out, gate_weight, up_weight, down_weight):
    pick_count = TOK_DEV * TOP
    slot_count = EXPERTS * CAP
    piece_width = FF // SPLIT
    blocks = D // 128
    device_ids = expert_ids.reshape(DEVICES, pick_count)
    onehot = (device_ids[:, :, None] == jnp.arange(EXPERTS, dtype=jnp.int32)[None, None, :]).astype(jnp.int32)
    before = jnp.cumsum(onehot, axis=1) - onehot
    slot_rank = jnp.sum(before * onehot, axis=2)
    slot_code = jnp.where(device_ids < EXPERTS, device_ids * CAP + slot_rank, -1)
    pick_table = (slot_code[:, :, None] == jnp.arange(slot_count, dtype=jnp.int32)[None, None, :]).astype(jnp.int32)
    slot_live = jnp.sum(pick_table, axis=1)
    local_pick = jnp.sum(pick_table * jnp.arange(pick_count, dtype=jnp.int32)[None, :, None], axis=1)
    device_base = (jnp.arange(DEVICES, dtype=jnp.int32) * pick_count)[:, None]
    global_pick = device_base + local_pick

    def by_expert(table_rows):
        return table_rows.reshape(DEVICES, EXPERTS, CAP).transpose(1, 0, 2).reshape(EXPERTS, DEVICES * CAP)

    pick_index = by_expert(global_pick).astype(jnp.int32)
    live_slots = by_expert(slot_live).astype(jnp.float32)

    values = tokens.astype(jnp.float32).reshape(TOKENS, blocks, 128)
    scales = (jnp.max(jnp.abs(values), axis=2) + 1e-6).astype(jnp.bfloat16)
    code_rows = (values / scales.astype(jnp.float32)[:, :, None]).astype(jnp.bfloat16).reshape(TOKENS, D)
    flat_weights = route_weights.reshape(-1)

    def expert_step(carry, inputs_now):
        mixed_acc, dx_acc, dw_acc = carry
        expert, picked, alive_mask = inputs_now
        token_rows = (picked // TOP).astype(jnp.int32)
        weight_rows = flat_weights[picked] * alive_mask
        decoded = code_rows[token_rows].astype(jnp.float32).reshape(-1, blocks, 128)
        decoded = decoded * scales[token_rows].astype(jnp.float32)[:, :, None]
        decoded = (decoded.reshape(-1, D) * alive_mask[:, None]).astype(jnp.bfloat16)
        cot_rows = grad_out[token_rows].astype(jnp.float32)
        grad_rows = (weight_rows[:, None] * cot_rows).astype(jnp.bfloat16)
        gate_slice = lax.dynamic_slice_in_dim(gate_weight, expert * FF, FF, 1)
        up_slice = lax.dynamic_slice_in_dim(up_weight, expert * FF, FF, 1)
        down_slice = lax.dynamic_slice_in_dim(down_weight, expert * FF, FF, 0)
        gate_pre = jnp.dot(decoded, gate_slice, preferred_element_type=jnp.float32)
        up_pre = jnp.dot(decoded, up_slice, preferred_element_type=jnp.float32)
        sigmoid_gate = jax.nn.sigmoid(gate_pre)
        silu_gate = gate_pre * sigmoid_gate
        hidden = (silu_gate * up_pre).astype(jnp.bfloat16)
        expert_out = jnp.zeros((DEVICES * CAP, D), jnp.float32)
        for piece_index in range(SPLIT):
            lower = piece_index * piece_width
            upper = lower + piece_width
            part_out = jnp.dot(hidden[:, lower:upper], down_slice[lower:upper], preferred_element_type=jnp.float32)
            expert_out = expert_out + part_out.astype(jnp.bfloat16).astype(jnp.float32)
        grad_down_e = jnp.dot(hidden.T, grad_rows, preferred_element_type=jnp.float32).astype(jnp.bfloat16)
        grad_hidden = jnp.dot(grad_rows, down_slice.T, preferred_element_type=jnp.float32)
        silu_slope = sigmoid_gate * (1.0 + gate_pre * (1.0 - sigmoid_gate))
        grad_gate_pre = (grad_hidden * up_pre * silu_slope).astype(jnp.bfloat16)
        grad_up_pre = (grad_hidden * silu_gate).astype(jnp.bfloat16)
        grad_gate_e = jnp.dot(decoded.T, grad_gate_pre, preferred_element_type=jnp.float32).astype(jnp.bfloat16)
        grad_up_e = jnp.dot(decoded.T, grad_up_pre, preferred_element_type=jnp.float32).astype(jnp.bfloat16)
        grad_in = jnp.zeros((DEVICES * CAP, D), jnp.float32)
        for piece_index in range(SPLIT):
            lower = piece_index * piece_width
            upper = lower + piece_width
            part_in = jnp.dot(grad_gate_pre[:, lower:upper], gate_slice[:, lower:upper].T, preferred_element_type=jnp.float32)
            part_in = part_in + jnp.dot(grad_up_pre[:, lower:upper], up_slice[:, lower:upper].T, preferred_element_type=jnp.float32)
            grad_in = grad_in + part_in.astype(jnp.bfloat16).astype(jnp.float32)
        mixed_acc = mixed_acc.at[token_rows].add(weight_rows[:, None] * expert_out)
        dx_acc = dx_acc.at[token_rows].add(alive_mask[:, None] * grad_in)
        dw_acc = dw_acc.at[picked].add(alive_mask * jnp.sum(cot_rows * expert_out, axis=1))
        return (mixed_acc, dx_acc, dw_acc), (grad_gate_e, grad_up_e, grad_down_e)

    start = (jnp.zeros((TOKENS, D), jnp.float32), jnp.zeros((TOKENS, D), jnp.float32), jnp.zeros((TOKENS * TOP,), jnp.float32))
    scanned = (jnp.arange(EXPERTS, dtype=jnp.int32), pick_index, live_slots)
    (mixed_acc, dx_acc, dw_acc), (grad_gate_all, grad_up_all, grad_down_all) = lax.scan(expert_step, start, scanned)
    mixed = mixed_acc.astype(jnp.bfloat16)
    grad_tokens = dx_acc.astype(jnp.bfloat16)
    grad_weights = dw_acc.reshape(TOKENS, TOP)
    grad_gate = grad_gate_all.transpose(1, 0, 2).reshape(D, EXPERTS * FF)
    grad_up = grad_up_all.transpose(1, 0, 2).reshape(D, EXPERTS * FF)
    grad_down = grad_down_all.reshape(EXPERTS * FF, D)
    return (mixed, grad_tokens, grad_weights, grad_gate, grad_up, grad_down)
```

```python
import functools

import jax
import jax.numpy as jnp
from jax import lax
from jax.experimental import pallas as pl
from jax.experimental.pallas import tpu as pltpu
from jax.sharding import PartitionSpec as P

F32 = jnp.float32
BF16 = jnp.bfloat16
MESH = pl.DeviceIdType.MESH

TOKENS = 128
TOP = 8
D = 7168
HID = 128
NX, NY, NZ = 4, 4, 4
EXPERTS = NX * NY
CAP = 5
PAD = 16
PACK = EXPERTS * PAD
HALF = EXPERTS * CAP
BLOCK = 2 * HALF
GROUP = NZ * BLOCK
ROWS = 2 * NZ * HALF
CW = 512
NQ = D // CW
AHEAD = 3
VMEM_LIMIT = 64 * 1024 * 1024 - 1024 * 1024


def dot(a, b):
    return jnp.dot(a, b, preferred_element_type=F32)


def dot_nt(a, b):
    return lax.dot_general(a, b, (((1,), (1,)), ((), ())), preferred_element_type=F32)


def kernel(
    ids_ref,
    weights_ref,
    tokens_hbm,
    cot_hbm,
    gate_hbm,
    up_hbm,
    down_hbm,
    mixed_hbm,
    dtok_hbm,
    dw_ref,
    dgate_hbm,
    dup_hbm,
    ddown_hbm,
    pack,
    inbox,
    gathered,
    wide,
    down,
    cot,
    sums,
    other,
    ring_lo,
    ring_hi,
    far_lo,
    far_hi,
    back,
    st_fin,
    st_down,
    st_wide,
    select,
    finish,
    row_scale,
    back_scale,
    pre,
    dhid,
    hid,
    dpre,
    hid_t,
    dpre_t,
    scores,
    load_sem,
    fs,
    fr,
    ags,
    ag_other,
    ag_lo,
    ag_hi,
    ag_far_lo,
    ag_far_hi,
    ps,
    pr,
    ss,
    rr_lo,
    rr_hi,
    rr_far_lo,
    rr_far_hi,
    ts,
    tr,
    fin_sem,
    grad_sem,
):
    x = lax.axis_index("node")
    local = lax.axis_index("local")
    y = local // (2 * NZ)
    z = (local // 2) % NZ
    c = local % 2
    z_up, z_dn, z_far = (z + 1) % NZ, (z + NZ - 1) % NZ, (z + 2) % NZ
    here = x * NY + y
    me = c * NZ + z
    partner = (x, y * 2 * NZ + z * 2 + (1 - c))
    up = (x, y * 2 * NZ + z_up * 2 + c)
    dn = (x, y * 2 * NZ + z_dn * 2 + c)

    def peer(k):
        px = (x + k // NY) % NX
        py = (y + k % NY) % NY
        return px * NY + py, (px, py * 2 * NZ + z * 2 + c)

    def load_copies(q):
        cols = pl.ds(pl.multiple_of(q * CW, CW), CW)
        return (
            pltpu.make_async_copy(
                tokens_hbm.at[:, cols], sums.at[pl.ds(pl.multiple_of(q * TOKENS, TOKENS), TOKENS)], load_sem.at[0, q]
            ),
            pltpu.make_async_copy(cot_hbm.at[:, cols], cot.at[q], load_sem.at[1, q]),
            pltpu.make_async_copy(down_hbm.at[:, cols], down.at[q], load_sem.at[2, q]),
        )

    gate_copy = pltpu.make_async_copy(gate_hbm, wide.at[:, pl.ds(0, HID)], load_sem.at[3, 0])
    up_copy = pltpu.make_async_copy(up_hbm, wide.at[:, pl.ds(HID, HID)], load_sem.at[3, 1])

    @pl.loop(0, NQ)
    def _(q):
        tok_copy, cot_copy, _ = load_copies(q)
        tok_copy.start()
        cot_copy.start()

    gate_copy.start()
    up_copy.start()

    @pl.loop(0, NQ)
    def _(q):
        load_copies(q)[2].start()

    barrier = pltpu.get_barrier_semaphore()

    @pl.loop(1, EXPERTS)
    def _(k):
        _, device = peer(k)
        pl.semaphore_signal(barrier, inc=1, device_id=device, device_id_type=MESH)

    for device in (partner, up, dn):
        pl.semaphore_signal(barrier, inc=1, device_id=device, device_id_type=MESH)

    ids = ids_ref[...]
    weights = weights_ref[...]
    row = lax.broadcasted_iota(jnp.int32, (TOKENS, PACK), 1)
    expert, place = row // PAD, row % PAD
    rank_of = jnp.where(place < CAP, place, jnp.where(place < 2 * CAP, place - CAP, -1)).astype(F32)
    named = jnp.zeros((TOKENS, PACK), F32)
    weight_of = jnp.zeros((TOKENS, PACK), F32)
    for k in range(TOP):
        hit = ids[:, k : k + 1] == expert
        named = jnp.where(hit, 1.0, named)
        weight_of = jnp.where(hit, weights[:, k : k + 1], weight_of)
    earlier = lax.broadcasted_iota(jnp.int32, (TOKENS, TOKENS), 1) < lax.broadcasted_iota(
        jnp.int32, (TOKENS, TOKENS), 0
    )
    rank = dot(jnp.where(earlier, 1.0, 0.0).astype(BF16), named.astype(BF16))
    chosen = jnp.where((named > 0.5) & (rank == rank_of), 1.0, 0.0)
    first = place < CAP
    fwd_t = jnp.where(first, chosen, 0.0)
    bwd_t = jnp.where(first, 0.0, chosen)
    finish[pl.ds(0, TOKENS), :] = fwd_t.astype(BF16)
    finish[pl.ds(TOKENS, TOKENS), :] = bwd_t.astype(BF16)
    select[:, pl.ds(0, TOKENS)] = fwd_t.T.astype(BF16)
    select[:, pl.ds(TOKENS, TOKENS)] = bwd_t.T.astype(BF16)
    slot_weight = jnp.sum((chosen * weight_of).T, axis=1, keepdims=True)
    row_place = lax.broadcasted_iota(jnp.int32, (PACK, 128), 0) % PAD
    slot_weight = jnp.broadcast_to(slot_weight, (PACK, 128))
    row_scale[...] = jnp.where(row_place < CAP, 1.0, slot_weight)
    back_scale[...] = jnp.where(row_place < CAP, slot_weight, 1.0)
    pre[...] = jnp.zeros_like(pre)
    dhid[...] = jnp.zeros_like(dhid)
    scores[...] = jnp.zeros_like(scores)

    def slot_target(shape, dim):
        r = lax.broadcasted_iota(jnp.int32, shape, dim)
        e, i = r // PAD, r % PAD
        return jnp.where(i < CAP, e * CAP + i, jnp.where(i < 2 * CAP, HALF + e * CAP + i - CAP, -1))

    def send_packets(q, dst, dst_at, send_sem, recv_sem):
        pltpu.make_async_copy(
            pack.at[q, pl.ds(pl.multiple_of(here * PAD, PAD), PAD)], dst_at(q, here), recv_sem.at[q]
        ).start()

        @pl.loop(1, EXPERTS)
        def _(k):
            e, device = peer(k)
            pltpu.make_async_remote_copy(
                src_ref=pack.at[q, pl.ds(pl.multiple_of(e * PAD, PAD), PAD)],
                dst_ref=dst_at(q, here),
                send_sem=send_sem.at[q],
                recv_sem=recv_sem.at[q],
                device_id=device,
                device_id_type=MESH,
            ).start()

    def inbox_at(q, e):
        return inbox.at[pl.ds(pl.multiple_of(q * PACK + e * PAD, PAD), PAD)]

    def back_at(q, e):
        return back.at[q, pl.ds(pl.multiple_of(e * PAD, PAD), PAD)]

    def wait_bytes(ref, sem):
        pltpu.make_async_copy(ref, ref, sem).wait()

    def wait_packet_sends(q, send_sem):
        wait_bytes(pack.at[q, pl.ds(0, PACK - PAD)], send_sem.at[q])

    def prepare(q):
        tok_copy, cot_copy, _ = load_copies(q)
        tok_copy.wait()
        cot_copy.wait()
        values = sums[pl.ds(pl.multiple_of(q * TOKENS, TOKENS), TOKENS), :].astype(F32)
        parts = []
        for b in range(CW // 128):
            v = values[:, b * 128 : (b + 1) * 128]
            scale = (jnp.max(jnp.abs(v), axis=1, keepdims=True) + 1e-06).astype(BF16).astype(F32)
            code = (v / scale).astype(BF16).astype(F32)
            parts.append((code * scale).astype(BF16))
        decoded = jnp.concatenate(parts, axis=1)
        source = jnp.concatenate([decoded, cot[q]], axis=0)
        picked = dot(select[...], source) * row_scale[:, 0:1]
        pack[q] = picked.astype(BF16)
        send_packets(q, inbox, inbox_at, fs, fr)

    pl.semaphore_wait(barrier, EXPERTS - 1 + 3)

    @pl.loop(0, AHEAD)
    def _(q):
        prepare(q)

    def remote(src, dst, send_sem, recv_sem, device):
        pltpu.make_async_remote_copy(
            src_ref=src, dst_ref=dst, send_sem=send_sem, recv_sem=recv_sem, device_id=device, device_id_type=MESH
        ).start()

    lower, upper = pl.ds(0, HALF), pl.ds(HALF, HALF)

    @pl.loop(0, NQ + 3)
    def _(t):
        @pl.when(t < NQ)
        def _():
            q = t
            wait_bytes(inbox.at[pl.ds(pl.multiple_of(q * PACK, PACK), PACK)], fr.at[q])
            compact = jnp.where(
                lax.broadcasted_iota(jnp.int32, (BLOCK, PACK), 0) == slot_target((BLOCK, PACK), 1), 1.0, 0.0
            ).astype(BF16)
            gathered[q, me] = dot(compact, inbox[pl.ds(pl.multiple_of(q * PACK, PACK), PACK), :]).astype(BF16)
            mine = gathered.at[q, me]
            remote(mine, mine, ags.at[q], ag_lo.at[q], up)
            remote(mine, mine, ags.at[q], ag_hi.at[q], dn)
            remote(mine, mine, ags.at[q], ag_other.at[q], partner)

        @pl.when((t >= 1) & (t < NQ + 1))
        def _():
            q = t - 1
            from_lo = gathered.at[q, c * NZ + z_dn]
            wait_bytes(from_lo, ag_lo.at[q])
            half = gathered.at[q, c * NZ + z_dn, lower]
            remote(half, half, ags.at[q], ag_far_lo.at[q], up)
            remote(from_lo, from_lo, ags.at[q], ag_other.at[q], partner)
            from_hi = gathered.at[q, c * NZ + z_up]
            wait_bytes(from_hi, ag_hi.at[q])
            half = gathered.at[q, c * NZ + z_up, upper]
            remote(half, half, ags.at[q], ag_far_hi.at[q], dn)
            remote(from_hi, from_hi, ags.at[q], ag_other.at[q], partner)

        @pl.when(t + AHEAD < NQ)
        def _():
            prepare(t + AHEAD)

        @pl.when((t >= 2) & (t < NQ + 2))
        def _():
            q = t - 2
            half = gathered.at[q, c * NZ + z_far, lower]
            wait_bytes(half, ag_far_lo.at[q])
            remote(half, half, ags.at[q], ag_other.at[q], partner)
            half = gathered.at[q, c * NZ + z_far, upper]
            wait_bytes(half, ag_far_hi.at[q])
            remote(half, half, ags.at[q], ag_other.at[q], partner)

        @pl.when(t == 3)
        def _():
            gate_copy.wait()
            up_copy.wait()

        @pl.when(t >= 3)
        def _():
            q = t - 3
            theirs = gathered.at[q, pl.ds((1 - c) * NZ, NZ)]
            wait_bytes(theirs, ag_other.at[q])
            load_copies(q)[2].wait()
            dec = gathered[q, :, 0:HALF, :].reshape(ROWS, CW)
            pre[...] += dot(dec, wide[pl.ds(pl.multiple_of(q * CW, CW), CW), :])
            grd = gathered[q, :, HALF:BLOCK, :].reshape(ROWS, CW)
            dhid[...] += dot_nt(grd, down[q])

    @pl.loop(0, ROWS // HID)
    def _(i):
        rows = pl.ds(pl.multiple_of(i * HID, HID), HID)
        gate_pre = pre[rows, 0:HID]
        up_pre = pre[rows, HID : 2 * HID]
        grad_hidden = dhid[rows, :]
        sig = 1.0 / (1.0 + jnp.exp(-gate_pre))
        silu = gate_pre * sig
        slope = sig * (1.0 + gate_pre * (1.0 - sig))
        hidden = (silu * up_pre).astype(BF16)
        d_gate = (grad_hidden * up_pre * slope).astype(BF16)
        d_up = (grad_hidden * silu).astype(BF16)
        hid[rows, :] = hidden
        dpre[rows, 0:HID] = d_gate
        dpre[rows, HID : 2 * HID] = d_up

    for i in range(ROWS // HID):
        rows = slice(i * HID, (i + 1) * HID)
        hid_t[:, rows] = hid[rows, :].astype(F32).T.astype(BF16)
        dpre_t[0:HID, rows] = dpre[rows, 0:HID].astype(F32).T.astype(BF16)
        dpre_t[HID : 2 * HID, rows] = dpre[rows, HID : 2 * HID].astype(F32).T.astype(BF16)

    @pl.loop(0, NQ)
    def _(q):
        wait_packet_sends(q, fs)
        wait_bytes(gathered.at[q, pl.ds(0, 7)], ags.at[q])

    def partial_rows(q, side, zz, size=BLOCK, offset=0):
        start = (q % 2) * 2 * GROUP + side * GROUP + zz * BLOCK + offset
        return pl.ds(pl.multiple_of(start, PAD), size)

    def other_rows(zz, size=BLOCK, offset=0):
        return pl.ds(pl.multiple_of(zz * BLOCK + offset, PAD), size)

    def sum_rows(q, k, size=BLOCK, offset=0):
        return pl.ds(pl.multiple_of((q % 4) * GROUP + k * BLOCK + offset, PAD), size)

    def grad_copies(q):
        slot = q % 2
        rows = pl.ds(pl.multiple_of(q * CW, CW), CW)
        return (
            pltpu.make_async_copy(st_down.at[slot], ddown_hbm.at[:, rows], grad_sem.at[0, slot]),
            pltpu.make_async_copy(st_wide.at[slot, :, pl.ds(0, HID)], dgate_hbm.at[rows], grad_sem.at[1, slot]),
            pltpu.make_async_copy(st_wide.at[slot, :, pl.ds(HID, HID)], dup_hbm.at[rows], grad_sem.at[2, slot]),
        )

    def fin_copies(q):
        slot = q % 2
        cols = pl.ds(pl.multiple_of(q * CW, CW), CW)
        return (
            pltpu.make_async_copy(st_fin.at[slot, pl.ds(0, TOKENS)], mixed_hbm.at[:, cols], fin_sem.at[0, slot]),
            pltpu.make_async_copy(st_fin.at[slot, pl.ds(TOKENS, TOKENS)], dtok_hbm.at[:, cols], fin_sem.at[1, slot]),
        )

    def pair_sum(q, zz, size, offset):
        mine = inbox[partial_rows(q, c, zz, size, offset), :].astype(F32)
        return mine + other[q, other_rows(zz, size, offset), :].astype(F32)

    @pl.loop(0, NQ + 4)
    def _(t):
        @pl.when(t < NQ)
        def _():
            q = t

            @pl.when(q >= 2)
            def _():
                wait_bytes(other.at[q - 2], ps.at[q - 2])

            out = dot(hid[...], down[q]).astype(BF16)
            dx = dot_nt(dpre[...], wide[pl.ds(pl.multiple_of(q * CW, CW), CW), :]).astype(BF16)
            for j in range(2 * NZ):
                base = (q % 2) * 2 * GROUP + j * BLOCK
                inbox[pl.ds(pl.multiple_of(base, PAD), HALF), :] = out[j * HALF : (j + 1) * HALF]
                inbox[pl.ds(pl.multiple_of(base + HALF, PAD), HALF), :] = dx[j * HALF : (j + 1) * HALF]
            remote(inbox.at[partial_rows(q, 1 - c, 0, GROUP)], other.at[q], ps.at[q], pr.at[q], partner)

        @pl.when((t >= 1) & (t < NQ + 1))
        def _():
            q = t - 1

            @pl.when(q >= 4)
            def _():
                wait_bytes(other.at[q - 4, pl.ds(0, GROUP - BLOCK)], ss.at[q - 4])

            wait_bytes(other.at[q], pr.at[q])
            sums[sum_rows(q, 0), :] = pair_sum(q, z_far, BLOCK, 0).astype(BF16)
            remote(sums.at[sum_rows(q, 0, HALF)], far_lo.at[q], ss.at[q], rr_far_lo.at[q], up)
            remote(sums.at[sum_rows(q, 0, HALF, HALF)], far_hi.at[q], ss.at[q], rr_far_hi.at[q], dn)
            sums[sum_rows(q, 1), :] = pair_sum(q, z_up, BLOCK, 0).astype(BF16)
            remote(sums.at[sum_rows(q, 1, HALF, HALF)], ring_lo.at[q, upper], ss.at[q], rr_lo.at[q], up)
            sums[sum_rows(q, 2), :] = pair_sum(q, z_dn, BLOCK, 0).astype(BF16)
            remote(sums.at[sum_rows(q, 2, HALF)], ring_hi.at[q, lower], ss.at[q], rr_hi.at[q], dn)
            sums[sum_rows(q, 3), :] = pair_sum(q, z, BLOCK, 0).astype(BF16)

        @pl.when((t >= 2) & (t < NQ + 2))
        def _():
            q = t - 2
            wait_bytes(far_lo.at[q], rr_far_lo.at[q])
            rows = sum_rows(q, 1, HALF)
            sums[rows, :] = (sums[rows, :].astype(F32) + far_lo[q].astype(F32)).astype(BF16)
            remote(sums.at[rows], ring_lo.at[q, lower], ss.at[q], rr_lo.at[q], up)
            wait_bytes(far_hi.at[q], rr_far_hi.at[q])
            rows = sum_rows(q, 2, HALF, HALF)
            sums[rows, :] = (sums[rows, :].astype(F32) + far_hi[q].astype(F32)).astype(BF16)
            remote(sums.at[rows], ring_hi.at[q, upper], ss.at[q], rr_hi.at[q], dn)

        @pl.when(t < NQ)
        def _():
            q = t

            @pl.when(q >= 2)
            def _():
                for copy in grad_copies(q - 2):
                    copy.wait()

            slot = q % 2
            dec = gathered[q, :, 0:HALF, :].reshape(ROWS, CW)
            grd = gathered[q, :, HALF:BLOCK, :].reshape(ROWS, CW)
            st_down[slot] = dot(hid_t[...], grd).astype(BF16)
            st_wide[slot] = dot(dpre_t[...], dec).T.astype(BF16)
            for copy in grad_copies(q):
                copy.start()

        @pl.when((t >= 3) & (t < NQ + 3))
        def _():
            q = t - 3
            wait_bytes(ring_lo.at[q], rr_lo.at[q])
            wait_bytes(ring_hi.at[q], rr_hi.at[q])
            total = (
                sums[sum_rows(q, 3), :].astype(F32) + ring_lo[q].astype(F32) + ring_hi[q].astype(F32)
            ).astype(BF16)
            expand = jnp.where(
                lax.broadcasted_iota(jnp.int32, (PACK, BLOCK), 1) == slot_target((PACK, BLOCK), 0), 1.0, 0.0
            ).astype(BF16)
            pack[q] = dot(expand, total).astype(BF16)
            send_packets(q, back, back_at, ts, tr)

        @pl.when(t >= 4)
        def _():
            q = t - 4
            slot = q % 2

            @pl.when(q >= 2)
            def _():
                for copy in fin_copies(q - 2):
                    copy.wait()

            wait_bytes(back.at[q], tr.at[q])
            rows = back[q]
            scaled = (rows.astype(F32) * back_scale[:, 0:1]).astype(BF16)
            st_fin[slot] = dot(finish[...], scaled).astype(BF16)
            scores[...] += dot_nt(cot[q], rows)
            for copy in fin_copies(q):
                copy.start()

    fwd = finish[pl.ds(0, TOKENS), :].astype(F32) * scores[...]
    for k in range(TOP):
        hit = ids_ref[:, k : k + 1] == expert
        dw_ref[:, k : k + 1] = jnp.sum(jnp.where(hit, fwd, 0.0), axis=1, keepdims=True)

    for q in (NQ - 2, NQ - 1):
        wait_bytes(other.at[q], ps.at[q])
        for copy in grad_copies(q) + fin_copies(q):
            copy.wait()
    for q in range(NQ - 4, NQ):
        wait_bytes(other.at[q, pl.ds(0, GROUP - BLOCK)], ss.at[q])

    @pl.loop(0, NQ)
    def _(q):
        wait_packet_sends(q, ts)


def on_device(tokens, expert_ids, route_weights, grad_out, gate_weight, up_weight, down_weight):
    any_spec = pl.BlockSpec(memory_space=pl.ANY)
    vmem_spec = pl.BlockSpec(memory_space=pltpu.VMEM)
    shape = jax.ShapeDtypeStruct
    dma = pltpu.SemaphoreType.DMA
    return pl.pallas_call(
        kernel,
        out_shape=(
            shape((TOKENS, D), BF16),
            shape((TOKENS, D), BF16),
            shape((TOKENS, TOP), F32),
            shape((D, HID), BF16),
            shape((D, HID), BF16),
            shape((HID, D), BF16),
        ),
        in_specs=[vmem_spec, vmem_spec] + [any_spec] * 5,
        out_specs=(any_spec, any_spec, vmem_spec, any_spec, any_spec, any_spec),
        scratch_shapes=[
            pltpu.VMEM((NQ, PACK, CW), BF16),
            pltpu.VMEM((NQ * PACK, CW), BF16),
            pltpu.VMEM((NQ, 2 * NZ, BLOCK, CW), BF16),
            pltpu.VMEM((D, 2 * HID), BF16),
            pltpu.VMEM((NQ, HID, CW), BF16),
            pltpu.VMEM((NQ, TOKENS, CW), BF16),
            pltpu.VMEM((4 * GROUP, CW), BF16),
            pltpu.VMEM((NQ, GROUP, CW), BF16),
            pltpu.VMEM((NQ, BLOCK, CW), BF16),
            pltpu.VMEM((NQ, BLOCK, CW), BF16),
            pltpu.VMEM((NQ, HALF, CW), BF16),
            pltpu.VMEM((NQ, HALF, CW), BF16),
            pltpu.VMEM((NQ, PACK, CW), BF16),
            pltpu.VMEM((2, 2 * TOKENS, CW), BF16),
            pltpu.VMEM((2, HID, CW), BF16),
            pltpu.VMEM((2, CW, 2 * HID), BF16),
            pltpu.VMEM((PACK, 2 * TOKENS), BF16),
            pltpu.VMEM((2 * TOKENS, PACK), BF16),
            pltpu.VMEM((PACK, 128), F32),
            pltpu.VMEM((PACK, 128), F32),
            pltpu.VMEM((ROWS, 2 * HID), F32),
            pltpu.VMEM((ROWS, HID), F32),
            pltpu.VMEM((ROWS, HID), BF16),
            pltpu.VMEM((ROWS, 2 * HID), BF16),
            pltpu.VMEM((HID, ROWS), BF16),
            pltpu.VMEM((2 * HID, ROWS), BF16),
            pltpu.VMEM((TOKENS, PACK), F32),
            dma((4, NQ)),
        ]
        + [dma((NQ,))] * 17
        + [dma((2, 2)), dma((3, 2))],
        compiler_params=pltpu.CompilerParams(
            collective_id=0, has_side_effects=True, vmem_limit_bytes=VMEM_LIMIT
        ),
        cost_estimate=pl.CostEstimate(
            flops=9 * 2 * ROWS * D * HID, bytes_accessed=10 * D * 256, transcendentals=ROWS * HID
        ),
        name="expert_layer",
    )(expert_ids, route_weights, tokens, grad_out, gate_weight, up_weight, down_weight)


def solution(mesh):
    rows = P(("node", "local"), None)
    cols = P(None, ("node", "local"))
    return jax.shard_map(
        on_device,
        mesh=mesh,
        in_specs=(rows, rows, rows, rows, cols, cols, rows),
        out_specs=(rows, rows, rows, cols, cols, rows),
        check_vma=False,
    )
```

```python
import functools

import jax
import jax.numpy as jnp
from jax import lax
from jax.experimental import pallas as pl
from jax.experimental.pallas import tpu as pltpu
from jax.sharding import PartitionSpec as P

F32 = jnp.float32
BF16 = jnp.bfloat16
MESH = pl.DeviceIdType.MESH

TOKENS = 128
TOP = 8
D = 7168
HID = 128
NX, NY, NZ = 4, 4, 4
EXPERTS = NX * NY
CAP = 5
PAD = 16
PACK = EXPERTS * PAD
HALF = EXPERTS * CAP
BLOCK = 2 * HALF
GROUP = NZ * BLOCK
ROWS = 2 * NZ * HALF
CW = 512
NQ = D // CW
NF = NQ // 2
AHEAD = 2
SPLITS = 2
PW = CW // SPLITS
BACK = 12
GRADS = NQ + 3
PARTS = 4
VMEM_LIMIT = 64 * 1024 * 1024 - 1024 * 1024


def dot(a, b):
    return jnp.dot(a, b, preferred_element_type=F32)


def dot_nt(a, b):
    return lax.dot_general(a, b, (((1,), (1,)), ((), ())), preferred_element_type=F32)


def kernel(
    ids_hbm,
    weights_hbm,
    tokens_hbm,
    cot_hbm,
    gate_hbm,
    up_hbm,
    down_hbm,
    mixed_hbm,
    dtok_hbm,
    dw_hbm,
    dgate_hbm,
    dup_hbm,
    ddown_hbm,
    pack,
    inbox,
    gathered,
    wide,
    down,
    cot,
    sums,
    other,
    ring_lo,
    ring_hi,
    far_lo,
    far_hi,
    back,
    st_fin,
    st_down,
    st_wide,
    ids_ref,
    weights_ref,
    dw_ref,
    chosen,
    select,
    finish,
    compact,
    expand,
    row_scale,
    pre,
    dhid,
    hid,
    dpre,
    hid_t,
    dpre_t,
    scores,
    load_sem,
    fs,
    fr,
    ags,
    ag_other,
    ag_lo,
    ag_hi,
    ag_far_lo,
    ag_far_hi,
    ps,
    pr,
    ss,
    rr_lo,
    rr_hi,
    rr_far_lo,
    rr_far_hi,
    ts,
    tr,
    fin_sem,
    grad_sem,
    first_sem,
    last_sem,
):
    x = lax.axis_index("node")
    local = lax.axis_index("local")
    y = local // (2 * NZ)
    z = (local // 2) % NZ
    c = local % 2
    z_up, z_dn, z_far = (z + 1) % NZ, (z + NZ - 1) % NZ, (z + 2) % NZ
    here = x * NY + y
    me = c * NZ + z
    partner = (x, y * 2 * NZ + z * 2 + (1 - c))
    up = (x, y * 2 * NZ + z_up * 2 + c)
    dn = (x, y * 2 * NZ + z_dn * 2 + c)

    def peer(k):
        px = (x + k // NY) % NX
        py = (y + k % NY) % NY
        return px * NY + py, (px, py * 2 * NZ + z * 2 + c)

    def cols_of(q):
        return pl.ds(pl.multiple_of(q * CW, CW), CW)

    def token_rows(q):
        return pl.ds(pl.multiple_of(q * TOKENS, TOKENS), TOKENS)

    def token_copy(q):
        return pltpu.make_async_copy(tokens_hbm.at[:, cols_of(q)], sums.at[token_rows(q)], load_sem.at[0, q])

    def cot_copy(q):
        return pltpu.make_async_copy(cot_hbm.at[:, cols_of(q)], cot.at[q], load_sem.at[1, q])

    def down_copy(q):
        return pltpu.make_async_copy(down_hbm.at[:, cols_of(q)], down.at[q], load_sem.at[2, q])

    ids_copy = pltpu.make_async_copy(ids_hbm, ids_ref, load_sem.at[3, 0])
    weights_copy = pltpu.make_async_copy(weights_hbm, weights_ref, load_sem.at[3, 1])
    gate_copy = pltpu.make_async_copy(gate_hbm, wide.at[:, pl.ds(0, HID)], load_sem.at[3, 2])
    up_copy = pltpu.make_async_copy(up_hbm, wide.at[:, pl.ds(HID, HID)], load_sem.at[3, 3])
    ids_copy.start()
    weights_copy.start()

    @pl.loop(0, NQ)
    def _(q):
        token_copy(q).start()

    gate_copy.start()
    up_copy.start()

    @pl.loop(0, NQ)
    def _(q):
        cot_copy(q).start()
        down_copy(q).start()

    barrier = pltpu.get_barrier_semaphore()

    @pl.loop(1, EXPERTS)
    def _(k):
        _, device = peer(k)
        pl.semaphore_signal(barrier, inc=1, device_id=device, device_id_type=MESH)

    for device in (partner, up, dn):
        pl.semaphore_signal(barrier, inc=1, device_id=device, device_id_type=MESH)

    ids_copy.wait()
    weights_copy.wait()
    row = lax.broadcasted_iota(jnp.int32, (PACK, TOKENS), 0)
    expert, place = row // PAD, row % PAD
    first = place < CAP
    rank_of = jnp.where(first, place, jnp.where(place < 2 * CAP, place - CAP, -1)).astype(F32)
    named = jnp.zeros((PACK, TOKENS), F32)
    weight_of = jnp.zeros((PACK, TOKENS), F32)
    for k in range(TOP):
        hit = ids_ref[k : k + 1, :] == expert
        named = jnp.where(hit, 1.0, named)
        weight_of = jnp.where(hit, weights_ref[k : k + 1, :], weight_of)
    earlier = lax.broadcasted_iota(jnp.int32, (TOKENS, TOKENS), 0) < lax.broadcasted_iota(
        jnp.int32, (TOKENS, TOKENS), 1
    )
    rank = dot(named.astype(BF16), jnp.where(earlier, 1.0, 0.0).astype(BF16))
    picks = jnp.where((named > 0.5) & (rank == rank_of), 1.0, 0.0)
    chosen[...] = picks
    even = jnp.where(first, picks, 0.0)
    odd = jnp.where(first, 0.0, picks)
    select[:, pl.ds(0, TOKENS)] = even.astype(BF16)
    select[:, pl.ds(TOKENS, TOKENS)] = odd.astype(BF16)
    row_scale[...] = jnp.broadcast_to(jnp.sum(picks * weight_of, axis=1, keepdims=True), (PACK, 128))

    def slot_target(shape, dim):
        r = lax.broadcasted_iota(jnp.int32, shape, dim)
        e, i = r // PAD, r % PAD
        return jnp.where(i < CAP, e * CAP + i, jnp.where(i < 2 * CAP, HALF + e * CAP + i - CAP, -1))

    def send_packets(q, dst_at, send_sem, recv_sem, cols=slice(None)):
        pltpu.make_async_copy(
            pack.at[q, pl.ds(pl.multiple_of(here * PAD, PAD), PAD), cols], dst_at(q, here, cols), recv_sem
        ).start()

        @pl.loop(1, EXPERTS)
        def _(k):
            e, device = peer(k)
            pltpu.make_async_remote_copy(
                src_ref=pack.at[q, pl.ds(pl.multiple_of(e * PAD, PAD), PAD), cols],
                dst_ref=dst_at(q, here, cols),
                send_sem=send_sem.at[q],
                recv_sem=recv_sem,
                device_id=device,
                device_id_type=MESH,
            ).start()

    def inbox_at(q, e, cols):
        return inbox.at[pl.ds(pl.multiple_of(q * PACK + e * PAD, PAD), PAD), cols]

    def back_at(q, e, cols):
        return back.at[q, pl.ds(pl.multiple_of(e * PAD, PAD), PAD), cols]

    def part_cols(p):
        return pl.ds(p * PW, PW)

    def wait_bytes(ref, sem):
        pltpu.make_async_copy(ref, ref, sem).wait()

    def wait_packet_sends(q, send_sem):
        wait_bytes(pack.at[q, pl.ds(0, PACK - PAD)], send_sem.at[q])

    def decode(q, cols=slice(None)):
        values = sums[token_rows(q), cols].astype(F32)
        parts = []
        for b in range(values.shape[1] // 128):
            v = values[:, b * 128 : (b + 1) * 128]
            scale = (jnp.max(jnp.abs(v), axis=1, keepdims=True) + 1e-06).astype(BF16).astype(F32)
            code = (v / scale).astype(BF16).astype(F32)
            parts.append((code * scale).astype(BF16))
        return jnp.concatenate(parts, axis=1)

    def prepare(q):
        @pl.when(q < NF)
        def _():
            token_copy(2 * q).wait()
            token_copy(2 * q + 1).wait()
            source = jnp.concatenate([decode(2 * q), decode(2 * q + 1)], axis=0)
            pack[q] = dot(select[...], source).astype(BF16)

        @pl.when(q >= NF)
        def _():
            k = q - NF
            cot_copy(2 * k).wait()
            cot_copy(2 * k + 1).wait()
            source = jnp.concatenate([cot[2 * k], cot[2 * k + 1]], axis=0)
            pack[q] = (dot(select[...], source) * row_scale[:, 0:1]).astype(BF16)

        send_packets(q, inbox_at, fs, fr.at[q])

    def remote(src, dst, send_sem, recv_sem, device):
        pltpu.make_async_remote_copy(
            src_ref=src, dst_ref=dst, send_sem=send_sem, recv_sem=recv_sem, device_id=device, device_id_type=MESH
        ).start()

    lower, upper = pl.ds(0, HALF), pl.ds(HALF, HALF)

    def activate():
        @pl.loop(0, ROWS // HID)
        def _(i):
            rows = pl.ds(pl.multiple_of(i * HID, HID), HID)
            gate_pre = pre[rows, 0:HID]
            sig = 1.0 / (1.0 + jnp.exp(-gate_pre))
            hid[rows, :] = (gate_pre * sig * pre[rows, HID : 2 * HID]).astype(BF16)

        for i in range(ROWS // HID):
            rows = slice(i * HID, (i + 1) * HID)
            hid_t[:, rows] = hid[rows, :].astype(F32).T.astype(BF16)

    def activate_back():
        @pl.loop(0, ROWS // HID)
        def _(i):
            rows = pl.ds(pl.multiple_of(i * HID, HID), HID)
            gate_pre = pre[rows, 0:HID]
            grad_hidden = dhid[rows, :]
            sig = 1.0 / (1.0 + jnp.exp(-gate_pre))
            slope = sig * (1.0 + gate_pre * (1.0 - sig))
            dpre[rows, 0:HID] = (grad_hidden * pre[rows, HID : 2 * HID] * slope).astype(BF16)
            dpre[rows, HID : 2 * HID] = (grad_hidden * (gate_pre * sig)).astype(BF16)

        for i in range(ROWS // HID):
            rows = slice(i * HID, (i + 1) * HID)
            dpre_t[0:HID, rows] = dpre[rows, 0:HID].astype(F32).T.astype(BF16)
            dpre_t[HID : 2 * HID, rows] = dpre[rows, HID : 2 * HID].astype(F32).T.astype(BF16)

    def partial_rows(q, side, zz, size=BLOCK, offset=0):
        start = (q % 2) * 2 * GROUP + side * GROUP + zz * BLOCK + offset
        return pl.ds(pl.multiple_of(start, PAD), size)

    def other_rows(zz, size=BLOCK, offset=0):
        return pl.ds(pl.multiple_of(zz * BLOCK + offset, PAD), size)

    def sum_rows(q, k, size=BLOCK, offset=0):
        return pl.ds(pl.multiple_of((q % 4) * GROUP + k * BLOCK + offset, PAD), size)

    def grad_copies(q):
        slot = q % 2
        rows = cols_of(q)
        return (
            pltpu.make_async_copy(st_down.at[slot], ddown_hbm.at[:, rows], grad_sem.at[0, slot]),
            pltpu.make_async_copy(st_wide.at[slot, :, pl.ds(0, HID)], dgate_hbm.at[rows], grad_sem.at[1, slot]),
            pltpu.make_async_copy(st_wide.at[slot, :, pl.ds(HID, HID)], dup_hbm.at[rows], grad_sem.at[2, slot]),
        )

    def fin_copies(q, out_hbm):
        slot = q % 2
        k = 2 * (q % NF)
        return (
            pltpu.make_async_copy(st_fin.at[slot, pl.ds(0, TOKENS)], out_hbm.at[:, cols_of(k)], fin_sem.at[0, slot]),
            pltpu.make_async_copy(
                st_fin.at[slot, pl.ds(TOKENS, TOKENS)], out_hbm.at[:, cols_of(k + 1)], fin_sem.at[1, slot]
            ),
        )

    def pair_sum(q, zz, size, offset):
        mine = inbox[partial_rows(q, c, zz, size, offset), :].astype(F32)
        return mine + other[q, other_rows(zz, size, offset), :].astype(F32)

    dw_copy = pltpu.make_async_copy(dw_ref, dw_hbm, load_sem.at[3, 0])

    token_copy(0).wait()
    token_copy(1).wait()
    for p in range(SPLITS):
        cols = part_cols(p)
        source = jnp.concatenate([decode(0, cols), decode(1, cols)], axis=0)
        pack[0, :, cols] = dot(select[...], source).astype(BF16)
        if p == 0:
            pl.semaphore_wait(barrier, EXPERTS - 1 + 3)
        send_packets(0, inbox_at, fs, first_sem.at[p], cols)
    compact[...] = jnp.where(
        lax.broadcasted_iota(jnp.int32, (BLOCK, PACK), 0) == slot_target((BLOCK, PACK), 1), 1.0, 0.0
    ).astype(BF16)
    prepare(1)
    for p in range(SPLITS):
        cols = part_cols(p)
        wait_bytes(inbox.at[pl.ds(0, PACK), cols], first_sem.at[p])
        gathered[0, me, :, cols] = dot(compact[...], inbox[pl.ds(0, PACK), cols]).astype(BF16)
        mine = gathered.at[0, me, :, cols]
        remote(mine, mine, ags.at[0], ag_lo.at[0], up)
        remote(mine, mine, ags.at[0], ag_hi.at[0], dn)
        remote(mine, mine, ags.at[0], ag_other.at[0], partner)
    prepare(2)
    finish[pl.ds(0, TOKENS), :] = jnp.where(first, chosen[...], 0.0).T.astype(BF16)
    finish[pl.ds(TOKENS, TOKENS), :] = jnp.where(first, 0.0, chosen[...]).T.astype(BF16)
    expand[...] = jnp.where(
        lax.broadcasted_iota(jnp.int32, (PACK, BLOCK), 1) == slot_target((PACK, BLOCK), 0), 1.0, 0.0
    ).astype(BF16)
    pre[...] = jnp.zeros_like(pre)
    dhid[...] = jnp.zeros_like(dhid)
    scores[...] = jnp.zeros_like(scores)

    @pl.loop(1, BACK + NQ + 4)
    def _(t):
        r = t - BACK

        @pl.when(t < NQ)
        def _():
            q = t
            wait_bytes(inbox.at[pl.ds(pl.multiple_of(q * PACK, PACK), PACK)], fr.at[q])
            gathered[q, me] = dot(compact[...], inbox[pl.ds(pl.multiple_of(q * PACK, PACK), PACK), :]).astype(BF16)
            mine = gathered.at[q, me]
            remote(mine, mine, ags.at[q], ag_lo.at[q], up)
            remote(mine, mine, ags.at[q], ag_hi.at[q], dn)
            remote(mine, mine, ags.at[q], ag_other.at[q], partner)

        @pl.when((t >= 1) & (t < NQ + 1))
        def _():
            q = t - 1
            from_lo = gathered.at[q, c * NZ + z_dn]
            wait_bytes(from_lo, ag_lo.at[q])
            half = gathered.at[q, c * NZ + z_dn, lower]
            remote(half, half, ags.at[q], ag_far_lo.at[q], up)
            remote(from_lo, from_lo, ags.at[q], ag_other.at[q], partner)
            from_hi = gathered.at[q, c * NZ + z_up]
            wait_bytes(from_hi, ag_hi.at[q])
            half = gathered.at[q, c * NZ + z_up, upper]
            remote(half, half, ags.at[q], ag_far_hi.at[q], dn)
            remote(from_hi, from_hi, ags.at[q], ag_other.at[q], partner)

        @pl.when(t + AHEAD < NQ)
        def _():
            prepare(t + AHEAD)

        @pl.when((t >= 2) & (t < NQ + 2))
        def _():
            q = t - 2
            half = gathered.at[q, c * NZ + z_far, lower]
            wait_bytes(half, ag_far_lo.at[q])
            remote(half, half, ags.at[q], ag_other.at[q], partner)
            half = gathered.at[q, c * NZ + z_far, upper]
            wait_bytes(half, ag_far_hi.at[q])
            remote(half, half, ags.at[q], ag_other.at[q], partner)

        @pl.when(t == 3)
        def _():
            gate_copy.wait()
            up_copy.wait()

        @pl.when((t >= 3) & (t < NQ + 3))
        def _():
            q = t - 3
            theirs = gathered.at[q, pl.ds((1 - c) * NZ, NZ)]
            wait_bytes(theirs, ag_other.at[q])
            rows_even = gathered[q, :, 0:HALF, :].reshape(ROWS, CW)
            rows_odd = gathered[q, :, HALF:BLOCK, :].reshape(ROWS, CW)

            @pl.when(q < NF)
            def _():
                pre[...] += dot(rows_even, wide[cols_of(2 * q), :]) + dot(rows_odd, wide[cols_of(2 * q + 1), :])

            @pl.when(q >= NF)
            def _():
                k = q - NF
                down_copy(2 * k).wait()
                down_copy(2 * k + 1).wait()
                dhid[...] += dot_nt(rows_even, down[2 * k]) + dot_nt(rows_odd, down[2 * k + 1])

            pl.when(q == NF - 1)(activate)
            pl.when(q == NQ - 1)(activate_back)

        @pl.when((r >= 0) & (r < NQ))
        def _():
            q = r

            @pl.when(q >= 2)
            def _():
                wait_bytes(other.at[q - 2], ps.at[q - 2])

            def keep(parts):
                for j in range(2 * NZ):
                    for h in range(2):
                        base = (q % 2) * 2 * GROUP + j * BLOCK + h * HALF
                        inbox[pl.ds(pl.multiple_of(base, PAD), HALF), :] = parts[h][j * HALF : (j + 1) * HALF]

            @pl.when(q < NF)
            def _():
                keep([dot(hid[...], down[2 * q + h]).astype(BF16) for h in range(2)])

            @pl.when(q >= NF)
            def _():
                keep([dot_nt(dpre[...], wide[cols_of(2 * (q - NF) + h), :]).astype(BF16) for h in range(2)])

            remote(inbox.at[partial_rows(q, 1 - c, 0, GROUP)], other.at[q], ps.at[q], pr.at[q], partner)

        @pl.when((r >= 1) & (r < NQ + 1))
        def _():
            q = r - 1

            @pl.when(q >= 4)
            def _():
                wait_bytes(other.at[q - 4, pl.ds(0, GROUP - BLOCK)], ss.at[q - 4])

            wait_bytes(other.at[q], pr.at[q])
            sums[sum_rows(q, 0), :] = pair_sum(q, z_far, BLOCK, 0).astype(BF16)
            remote(sums.at[sum_rows(q, 0, HALF)], far_lo.at[q], ss.at[q], rr_far_lo.at[q], up)
            remote(sums.at[sum_rows(q, 0, HALF, HALF)], far_hi.at[q], ss.at[q], rr_far_hi.at[q], dn)
            sums[sum_rows(q, 1), :] = pair_sum(q, z_up, BLOCK, 0).astype(BF16)
            remote(sums.at[sum_rows(q, 1, HALF, HALF)], ring_lo.at[q, upper], ss.at[q], rr_lo.at[q], up)
            sums[sum_rows(q, 2), :] = pair_sum(q, z_dn, BLOCK, 0).astype(BF16)
            remote(sums.at[sum_rows(q, 2, HALF)], ring_hi.at[q, lower], ss.at[q], rr_hi.at[q], dn)
            sums[sum_rows(q, 3), :] = pair_sum(q, z, BLOCK, 0).astype(BF16)

        @pl.when((r >= 2) & (r < NQ + 2))
        def _():
            q = r - 2
            wait_bytes(far_lo.at[q], rr_far_lo.at[q])
            rows = sum_rows(q, 1, HALF)
            sums[rows, :] = (sums[rows, :].astype(F32) + far_lo[q].astype(F32)).astype(BF16)
            remote(sums.at[rows], ring_lo.at[q, lower], ss.at[q], rr_lo.at[q], up)
            wait_bytes(far_hi.at[q], rr_far_hi.at[q])
            rows = sum_rows(q, 2, HALF, HALF)
            sums[rows, :] = (sums[rows, :].astype(F32) + far_hi[q].astype(F32)).astype(BF16)
            remote(sums.at[rows], ring_hi.at[q, upper], ss.at[q], rr_hi.at[q], dn)

        @pl.when((r >= 3) & (r < NQ + 3))
        def _():
            q = r - 3
            wait_bytes(ring_lo.at[q], rr_lo.at[q])
            wait_bytes(ring_hi.at[q], rr_hi.at[q])
            wait_packet_sends(q, fs)
            wait_bytes(gathered.at[q, pl.ds(0, 7)], ags.at[q])

            def total(cols):
                return (
                    sums[sum_rows(q, 3), cols].astype(F32)
                    + ring_lo[q, :, cols].astype(F32)
                    + ring_hi[q, :, cols].astype(F32)
                ).astype(BF16)

            @pl.when(q < NQ - 1)
            def _():
                pack[q] = dot(expand[...], total(slice(None))).astype(BF16)
                send_packets(q, back_at, ts, tr.at[q])

            @pl.when(q == NQ - 1)
            def _():
                for p in range(SPLITS):
                    cols = part_cols(p)
                    pack[q, :, cols] = dot(expand[...], total(cols)).astype(BF16)
                    send_packets(q, back_at, ts, last_sem.at[p], cols)

        @pl.when((r >= 4) & (r < NQ + 4))
        def _():
            q = r - 4
            slot = q % 2

            @pl.when(q >= 2)
            def _():
                for copy in fin_copies(q - 2, mixed_hbm):
                    copy.wait()

            @pl.when(q < NQ - 1)
            def _():
                wait_bytes(back.at[q], tr.at[q])

            @pl.when(q >= 1)
            def _():
                wait_packet_sends(q - 1, ts)

            @pl.when(q < NF)
            def _():
                rows = back[q]
                scaled = (rows.astype(F32) * row_scale[:, 0:1]).astype(BF16)
                st_fin[slot] = dot(finish[...], scaled).astype(BF16)
                is_first = lax.broadcasted_iota(jnp.int32, (PACK, TOKENS), 0) % PAD < CAP
                scores[...] += jnp.where(is_first, dot_nt(rows, cot[2 * q]), dot_nt(rows, cot[2 * q + 1]))
                for copy in fin_copies(q, mixed_hbm):
                    copy.start()

            @pl.when((q >= NF) & (q < NQ - 1))
            def _():
                st_fin[slot] = dot(finish[...], back[q]).astype(BF16)
                for copy in fin_copies(q, dtok_hbm):
                    copy.start()

            @pl.when(q == NQ - 1)
            def _():
                for p in range(SPLITS):
                    cols = part_cols(p)
                    wait_bytes(back.at[q, :, cols], last_sem.at[p])
                    st_fin[slot, :, cols] = dot(finish[...], back[q, :, cols]).astype(BF16)
                for copy in fin_copies(q, dtok_hbm):
                    copy.start()

            @pl.when(q == NF)
            def _():
                by_slot = chosen[...] * scores[...]
                for k in range(TOP):
                    hit = ids_ref[k : k + 1, :] == lax.broadcasted_iota(jnp.int32, (PACK, TOKENS), 0) // PAD
                    dw_ref[k : k + 1, :] = jnp.sum(jnp.where(hit, by_slot, 0.0), axis=0, keepdims=True)
                dw_copy.start()

        for h in range(2):

            @pl.when((t >= GRADS) & (t < GRADS + NF))
            def _():
                g = t - GRADS
                q = 2 * g + h

                @pl.when(q >= 2)
                def _():
                    for copy in grad_copies(q - 2):
                        copy.wait()

                dec = gathered[g, :, h * HALF : (h + 1) * HALF, :].reshape(ROWS, CW)
                grd = gathered[NF + g, :, h * HALF : (h + 1) * HALF, :].reshape(ROWS, CW)
                st_down[h] = dot(hid_t[...], grd).astype(BF16)
                st_wide[h] = dot(dpre_t[...], dec).T.astype(BF16)
                for copy in grad_copies(q):
                    copy.start()

    for q in (NQ - 2, NQ - 1):
        wait_bytes(other.at[q], ps.at[q])
        for copy in grad_copies(q) + fin_copies(q, dtok_hbm):
            copy.wait()
    for q in range(NQ - 4, NQ):
        wait_bytes(other.at[q, pl.ds(0, GROUP - BLOCK)], ss.at[q])

    wait_packet_sends(NQ - 1, ts)
    dw_copy.wait()


def copy_out(*refs):
    count = (len(refs) - 2) // 3
    sources, results, held = refs[:count], refs[count : 2 * count], refs[2 * count : 3 * count]
    in_sem, out_sem = refs[3 * count :]
    reads, writes = [], []
    for i in range(count):
        rows = held[i].shape[0] // PARTS
        for p in range(PARTS if rows >= 16 else 1):
            part = pl.ds(p * rows, rows) if rows >= 16 else pl.ds(0, held[i].shape[0])
            reads.append(pltpu.make_async_copy(sources[i].at[part], held[i].at[part], in_sem.at[i, p]))
            writes.append(pltpu.make_async_copy(held[i].at[part], results[i].at[part], out_sem.at[i, p]))
    for copy in reads:
        copy.start()
    for read, write in zip(reads, writes):
        read.wait()
        write.start()
    for copy in writes:
        copy.wait()


def on_device(tokens, expert_ids, route_weights, grad_out, gate_weight, up_weight, down_weight):
    any_spec = pl.BlockSpec(memory_space=pl.ANY)
    shape = jax.ShapeDtypeStruct
    dma = pltpu.SemaphoreType.DMA
    outs = (
        shape((TOKENS, D), BF16),
        shape((TOKENS, D), BF16),
        shape((TOP, TOKENS), F32),
        shape((D, HID), BF16),
        shape((D, HID), BF16),
        shape((HID, D), BF16),
    )
    results = pl.pallas_call(
        kernel,
        out_shape=outs,
        in_specs=[any_spec] * 7,
        out_specs=(any_spec,) * 6,
        scratch_shapes=[
            pltpu.VMEM((NQ, PACK, CW), BF16),
            pltpu.VMEM((NQ * PACK, CW), BF16),
            pltpu.VMEM((NQ, 2 * NZ, BLOCK, CW), BF16),
            pltpu.VMEM((D, 2 * HID), BF16),
            pltpu.VMEM((NQ, HID, CW), BF16),
            pltpu.VMEM((NQ, TOKENS, CW), BF16),
            pltpu.VMEM((4 * GROUP, CW), BF16),
            pltpu.VMEM((NQ, GROUP, CW), BF16),
            pltpu.VMEM((NQ, BLOCK, CW), BF16),
            pltpu.VMEM((NQ, BLOCK, CW), BF16),
            pltpu.VMEM((NQ, HALF, CW), BF16),
            pltpu.VMEM((NQ, HALF, CW), BF16),
            pltpu.VMEM((NQ, PACK, CW), BF16),
            pltpu.VMEM((2, 2 * TOKENS, CW), BF16),
            pltpu.VMEM((2, HID, CW), BF16),
            pltpu.VMEM((2, CW, 2 * HID), BF16),
            pltpu.VMEM((TOP, TOKENS), jnp.int32),
            pltpu.VMEM((TOP, TOKENS), F32),
            pltpu.VMEM((TOP, TOKENS), F32),
            pltpu.VMEM((PACK, TOKENS), F32),
            pltpu.VMEM((PACK, 2 * TOKENS), BF16),
            pltpu.VMEM((2 * TOKENS, PACK), BF16),
            pltpu.VMEM((BLOCK, PACK), BF16),
            pltpu.VMEM((PACK, BLOCK), BF16),
            pltpu.VMEM((PACK, 128), F32),
            pltpu.VMEM((ROWS, 2 * HID), F32),
            pltpu.VMEM((ROWS, HID), F32),
            pltpu.VMEM((ROWS, HID), BF16),
            pltpu.VMEM((ROWS, 2 * HID), BF16),
            pltpu.VMEM((HID, ROWS), BF16),
            pltpu.VMEM((2 * HID, ROWS), BF16),
            pltpu.VMEM((PACK, TOKENS), F32),
            dma((4, NQ)),
        ]
        + [dma((NQ,))] * 17
        + [dma((2, 2)), dma((3, 2)), dma((SPLITS,)), dma((SPLITS,))],
        compiler_params=pltpu.CompilerParams(
            collective_id=0, has_side_effects=True, vmem_limit_bytes=VMEM_LIMIT
        ),
        cost_estimate=pl.CostEstimate(
            flops=9 * 2 * ROWS * D * HID, bytes_accessed=10 * D * 256, transcendentals=ROWS * HID
        ),
        name="expert_layer",
    )(expert_ids.T, route_weights.T, tokens, grad_out, gate_weight, up_weight, down_weight)
    mixed, dtok, dw, dgate, dup, ddown = pl.pallas_call(
        copy_out,
        out_shape=outs,
        in_specs=[any_spec] * 6,
        out_specs=(any_spec,) * 6,
        scratch_shapes=[pltpu.VMEM(o.shape, o.dtype) for o in outs] + [dma((6, PARTS)), dma((6, PARTS))],
        compiler_params=pltpu.CompilerParams(vmem_limit_bytes=VMEM_LIMIT),
        name="copy_out",
    )(*results)
    return (mixed, dtok, dw.T, dgate, dup, ddown)


def solution(mesh):
    rows = P(("node", "local"), None)
    cols = P(None, ("node", "local"))
    return jax.shard_map(
        on_device,
        mesh=mesh,
        in_specs=(rows, rows, rows, rows, cols, cols, rows),
        out_specs=(rows, rows, rows, cols, cols, rows),
        check_vma=False,
    )
```

```python
import functools

import jax
import jax.numpy as jnp
from jax import lax
from jax.experimental import pallas as pl
from jax.experimental.pallas import tpu as pltpu
from jax.sharding import PartitionSpec as P

F32 = jnp.float32
BF16 = jnp.bfloat16
MESH = pl.DeviceIdType.MESH

TOKENS = 128
TOP = 8
D = 7168
HID = 128
NX, NY, NZ = 4, 4, 4
EXPERTS = NX * NY
CAP = 5
PAD = 16
SEGS = 3
PACK = EXPERTS * PAD
HALF = EXPERTS * CAP
BLOCK = 2 * HALF
GROUP = NZ * BLOCK
ROWS = 2 * NZ * HALF
CW = 512
NQ = D // CW
NF = NQ // 2
AHEAD = 2
PAIR = 2 * CW
SEG = 384
BACK = 12
GRADS = NQ + 3
PARTS = 4
VMEM_LIMIT = 64 * 1024 * 1024 - 1024 * 1024


def dot(a, b):
    return jnp.dot(a, b, preferred_element_type=F32)


def dot_nt(a, b):
    return lax.dot_general(a, b, (((1,), (1,)), ((), ())), preferred_element_type=F32)


def kernel(
    ids_hbm,
    weights_hbm,
    tokens_hbm,
    cot_hbm,
    gate_hbm,
    up_hbm,
    down_hbm,
    mixed_hbm,
    dtok_hbm,
    dw_hbm,
    dgate_hbm,
    dup_hbm,
    ddown_hbm,
    pack,
    inbox,
    partial,
    gathered,
    wide,
    down,
    cot,
    sums,
    other,
    ring_lo,
    ring_hi,
    far_lo,
    far_hi,
    back,
    st_fin,
    st_down,
    st_wide,
    ids_ref,
    weights_ref,
    dw_ref,
    chosen,
    select,
    finish,
    compact,
    expand,
    row_scale,
    pre,
    dhid,
    hid,
    dpre,
    hid_t,
    dpre_t,
    scores,
    load_sem,
    fs,
    fr,
    ags,
    ag_other,
    ag_lo,
    ag_hi,
    ag_far_lo,
    ag_far_hi,
    ps,
    pr,
    ss,
    rr_lo,
    rr_hi,
    rr_far_lo,
    rr_far_hi,
    ts,
    tr,
    fin_sem,
    grad_sem,
):
    x = lax.axis_index("node")
    local = lax.axis_index("local")
    y = local // (2 * NZ)
    z = (local // 2) % NZ
    c = local % 2
    z_up, z_dn, z_far = (z + 1) % NZ, (z + NZ - 1) % NZ, (z + 2) % NZ
    here = x * NY + y
    me = c * NZ + z
    partner = (x, y * 2 * NZ + z * 2 + (1 - c))
    up = (x, y * 2 * NZ + z_up * 2 + c)
    dn = (x, y * 2 * NZ + z_dn * 2 + c)

    def peer(k):
        px = (x + k // NY) % NX
        py = (y + k % NY) % NY
        return px * NY + py, (px, py * 2 * NZ + z * 2 + c)

    def cols_of(q):
        return pl.ds(pl.multiple_of(q * CW, CW), CW)

    def pair_of(q):
        return pl.ds(pl.multiple_of(q * PAIR, PAIR), PAIR)

    def token_rows(q):
        return pl.ds(pl.multiple_of(q * TOKENS, TOKENS), TOKENS)

    def token_copy(q):
        return pltpu.make_async_copy(tokens_hbm.at[:, cols_of(q)], sums.at[token_rows(q)], load_sem.at[0, q])

    def cot_copy(q):
        return pltpu.make_async_copy(cot_hbm.at[:, pair_of(q)], cot.at[q], load_sem.at[1, q])

    def down_copy(q):
        return pltpu.make_async_copy(down_hbm.at[:, cols_of(q)], down.at[q], load_sem.at[2, q])

    ids_copy = pltpu.make_async_copy(ids_hbm, ids_ref, load_sem.at[3, 0])
    weights_copy = pltpu.make_async_copy(weights_hbm, weights_ref, load_sem.at[3, 1])
    gate_copy = pltpu.make_async_copy(gate_hbm, wide.at[:, pl.ds(0, HID)], load_sem.at[3, 2])
    up_copy = pltpu.make_async_copy(up_hbm, wide.at[:, pl.ds(HID, HID)], load_sem.at[3, 3])
    ids_copy.start()
    weights_copy.start()

    @pl.loop(0, NQ)
    def _(q):
        token_copy(q).start()

    gate_copy.start()
    up_copy.start()

    @pl.loop(0, NF)
    def _(q):
        cot_copy(q).start()
        down_copy(2 * q).start()
        down_copy(2 * q + 1).start()

    barrier = pltpu.get_barrier_semaphore()

    @pl.loop(1, EXPERTS)
    def _(k):
        _, device = peer(k)
        pl.semaphore_signal(barrier, inc=1, device_id=device, device_id_type=MESH)

    for device in (partner, up, dn):
        pl.semaphore_signal(barrier, inc=1, device_id=device, device_id_type=MESH)

    ids_copy.wait()
    weights_copy.wait()
    row = lax.broadcasted_iota(jnp.int32, (PACK, TOKENS), 0)
    expert, place = row // PAD, row % PAD
    segment = place // CAP
    rank_of = jnp.where(segment < SEGS, place % CAP, -1).astype(F32)
    named = jnp.zeros((PACK, TOKENS), F32)
    weight_of = jnp.zeros((PACK, TOKENS), F32)
    for k in range(TOP):
        hit = ids_ref[k : k + 1, :] == expert
        named = jnp.where(hit, 1.0, named)
        weight_of = jnp.where(hit, weights_ref[k : k + 1, :], weight_of)
    earlier = lax.broadcasted_iota(jnp.int32, (TOKENS, TOKENS), 0) < lax.broadcasted_iota(
        jnp.int32, (TOKENS, TOKENS), 1
    )
    rank = dot(named.astype(BF16), jnp.where(earlier, 1.0, 0.0).astype(BF16))
    picks = jnp.where((named > 0.5) & (rank == rank_of), 1.0, 0.0)
    chosen[...] = picks
    for k in range(SEGS):
        select[:, pl.ds(k * TOKENS, TOKENS)] = jnp.where(segment == k, picks, 0.0).astype(BF16)
    row_scale[...] = jnp.broadcast_to(jnp.sum(picks * weight_of, axis=1, keepdims=True), (PACK, 128))

    def slot_target(shape, dim):
        r = lax.broadcasted_iota(jnp.int32, shape, dim)
        e, i = r // PAD, r % PAD
        return jnp.where(i < SEGS * CAP, (i // CAP) * HALF + e * CAP + i % CAP, -1)

    def send_packets(q, dst_at, send_sem, recv_sem):
        pltpu.make_async_copy(
            pack.at[q, pl.ds(pl.multiple_of(here * PAD, PAD), PAD)], dst_at(q, here), recv_sem
        ).start()

        @pl.loop(1, EXPERTS)
        def _(k):
            e, device = peer(k)
            pltpu.make_async_remote_copy(
                src_ref=pack.at[q, pl.ds(pl.multiple_of(e * PAD, PAD), PAD)],
                dst_ref=dst_at(q, here),
                send_sem=send_sem.at[q],
                recv_sem=recv_sem,
                device_id=device,
                device_id_type=MESH,
            ).start()

    def inbox_at(q, e):
        return inbox.at[q, pl.ds(pl.multiple_of(e * PAD, PAD), PAD)]

    def back_at(q, e):
        return back.at[q, pl.ds(pl.multiple_of(e * PAD, PAD), PAD)]

    def wait_bytes(ref, sem):
        pltpu.make_async_copy(ref, ref, sem).wait()

    def wait_packet_sends(q, send_sem):
        wait_bytes(pack.at[q, pl.ds(0, PACK - PAD)], send_sem.at[q])

    def decode(q):
        token_copy(q).wait()
        values = sums[token_rows(q), :].astype(F32)
        parts = []
        for b in range(CW // 128):
            v = values[:, b * 128 : (b + 1) * 128]
            scale = (jnp.max(jnp.abs(v), axis=1, keepdims=True) + 1e-06).astype(BF16).astype(F32)
            code = (v / scale).astype(BF16).astype(F32)
            parts.append((code * scale).astype(BF16))
        return parts

    def segments(rows):
        short = rows[:, 2 * SEG :]
        zeros = jnp.zeros((rows.shape[0], SEGS * SEG - PAIR), BF16)
        return jnp.concatenate([rows[:, :SEG], rows[:, SEG : 2 * SEG], jnp.concatenate([short, zeros], axis=1)], axis=0)

    def prepare(q):
        @pl.when(q < NF)
        def _():
            decoded = jnp.concatenate(decode(2 * q) + decode(2 * q + 1), axis=1)
            pack[q] = dot(select[...], segments(decoded)).astype(BF16)

        @pl.when(q >= NF)
        def _():
            cot_copy(q - NF).wait()
            pack[q] = (dot(select[...], segments(cot[q - NF])) * row_scale[:, 0:1]).astype(BF16)

    def send_forward(q):
        send_packets(q, inbox_at, fs, fr.at[q])

    def remote(src, dst, send_sem, recv_sem, device):
        pltpu.make_async_remote_copy(
            src_ref=src, dst_ref=dst, send_sem=send_sem, recv_sem=recv_sem, device_id=device, device_id_type=MESH
        ).start()

    lower, upper = pl.ds(0, HALF), pl.ds(HALF, HALF)

    def activate():
        @pl.loop(0, ROWS // HID)
        def _(i):
            rows = pl.ds(pl.multiple_of(i * HID, HID), HID)
            gate_pre = pre[rows, 0:HID]
            sig = 1.0 / (1.0 + jnp.exp(-gate_pre))
            hid[rows, :] = (gate_pre * sig * pre[rows, HID : 2 * HID]).astype(BF16)

        for i in range(ROWS // HID):
            rows = slice(i * HID, (i + 1) * HID)
            hid_t[:, rows] = hid[rows, :].astype(F32).T.astype(BF16)

    def activate_back():
        @pl.loop(0, ROWS // HID)
        def _(i):
            rows = pl.ds(pl.multiple_of(i * HID, HID), HID)
            gate_pre = pre[rows, 0:HID]
            grad_hidden = dhid[rows, :]
            sig = 1.0 / (1.0 + jnp.exp(-gate_pre))
            slope = sig * (1.0 + gate_pre * (1.0 - sig))
            dpre[rows, 0:HID] = (grad_hidden * pre[rows, HID : 2 * HID] * slope).astype(BF16)
            dpre[rows, HID : 2 * HID] = (grad_hidden * (gate_pre * sig)).astype(BF16)

        for i in range(ROWS // HID):
            rows = slice(i * HID, (i + 1) * HID)
            dpre_t[0:HID, rows] = dpre[rows, 0:HID].astype(F32).T.astype(BF16)
            dpre_t[HID : 2 * HID, rows] = dpre[rows, HID : 2 * HID].astype(F32).T.astype(BF16)

    def partial_rows(q, side, zz, size=BLOCK, offset=0):
        start = (q % 2) * 2 * GROUP + side * GROUP + zz * BLOCK + offset
        return pl.ds(pl.multiple_of(start, PAD), size)

    def other_rows(zz, size=BLOCK, offset=0):
        return pl.ds(pl.multiple_of(zz * BLOCK + offset, PAD), size)

    def sum_rows(q, k, size=BLOCK, offset=0):
        return pl.ds(pl.multiple_of((q % 4) * GROUP + k * BLOCK + offset, PAD), size)

    def grad_copies(q):
        slot = q % 2
        rows = cols_of(q)
        return (
            pltpu.make_async_copy(st_down.at[slot], ddown_hbm.at[:, rows], grad_sem.at[0, slot]),
            pltpu.make_async_copy(st_wide.at[slot, :, pl.ds(0, HID)], dgate_hbm.at[rows], grad_sem.at[1, slot]),
            pltpu.make_async_copy(st_wide.at[slot, :, pl.ds(HID, HID)], dup_hbm.at[rows], grad_sem.at[2, slot]),
        )

    def fin_copy(q, out_hbm):
        slot = q % 2
        return pltpu.make_async_copy(st_fin.at[slot], out_hbm.at[:, pair_of(q % NF)], fin_sem.at[slot])

    def pair_sum(q, zz, size, offset):
        mine = partial[partial_rows(q, c, zz, size, offset), :].astype(F32)
        return mine + other[q, other_rows(zz, size, offset), :].astype(F32)

    dw_copy = pltpu.make_async_copy(dw_ref, dw_hbm, load_sem.at[3, 0])

    def keep_own(q):
        wait_bytes(inbox.at[q], fr.at[q])
        kept = dot(compact[...], inbox[q]).astype(BF16)
        gathered[q, me, 0:HALF, 0:SEG] = kept[0:HALF]
        gathered[q, me, 0:HALF, SEG:CW] = kept[HALF : 2 * HALF, 0 : CW - SEG]
        gathered[q, me, HALF:BLOCK, 0 : 2 * SEG - CW] = kept[HALF : 2 * HALF, CW - SEG : SEG]
        gathered[q, me, HALF:BLOCK, 2 * SEG - CW : CW] = kept[2 * HALF :, 0 : PAIR - 2 * SEG]
        mine = gathered.at[q, me]
        remote(mine, mine, ags.at[q], ag_lo.at[q], up)
        remote(mine, mine, ags.at[q], ag_hi.at[q], dn)
        remote(mine, mine, ags.at[q], ag_other.at[q], partner)

    prepare(0)
    pl.semaphore_wait(barrier, EXPERTS - 1 + 3)
    send_forward(0)
    compact[...] = jnp.where(
        lax.broadcasted_iota(jnp.int32, (SEGS * HALF, PACK), 0) == slot_target((SEGS * HALF, PACK), 1), 1.0, 0.0
    ).astype(BF16)
    prepare(1)
    send_forward(1)
    keep_own(0)
    prepare(2)
    send_forward(2)
    for k in range(SEGS):
        finish[pl.ds(k * TOKENS, TOKENS), :] = jnp.where(segment == k, chosen[...], 0.0).T.astype(BF16)
    expand[...] = jnp.where(
        lax.broadcasted_iota(jnp.int32, (PACK, SEGS * HALF), 1) == slot_target((PACK, SEGS * HALF), 0), 1.0, 0.0
    ).astype(BF16)
    pre[...] = jnp.zeros_like(pre)
    dhid[...] = jnp.zeros_like(dhid)
    scores[...] = jnp.zeros_like(scores)

    @pl.loop(1, BACK + NQ + 4)
    def _(t):
        r = t - BACK

        @pl.when(t < NQ)
        def _():
            keep_own(t)

        @pl.when((t >= 1) & (t < NQ + 1))
        def _():
            q = t - 1
            from_lo = gathered.at[q, c * NZ + z_dn]
            wait_bytes(from_lo, ag_lo.at[q])
            half = gathered.at[q, c * NZ + z_dn, lower]
            remote(half, half, ags.at[q], ag_far_lo.at[q], up)
            remote(from_lo, from_lo, ags.at[q], ag_other.at[q], partner)
            from_hi = gathered.at[q, c * NZ + z_up]
            wait_bytes(from_hi, ag_hi.at[q])
            half = gathered.at[q, c * NZ + z_up, upper]
            remote(half, half, ags.at[q], ag_far_hi.at[q], dn)
            remote(from_hi, from_hi, ags.at[q], ag_other.at[q], partner)

        @pl.when(t + AHEAD < NQ)
        def _():
            prepare(t + AHEAD)
            send_forward(t + AHEAD)

        @pl.when((t >= 2) & (t < NQ + 2))
        def _():
            q = t - 2
            half = gathered.at[q, c * NZ + z_far, lower]
            wait_bytes(half, ag_far_lo.at[q])
            remote(half, half, ags.at[q], ag_other.at[q], partner)
            half = gathered.at[q, c * NZ + z_far, upper]
            wait_bytes(half, ag_far_hi.at[q])
            remote(half, half, ags.at[q], ag_other.at[q], partner)

        @pl.when(t == 3)
        def _():
            gate_copy.wait()
            up_copy.wait()

        @pl.when((t >= 3) & (t < NQ + 3))
        def _():
            q = t - 3
            theirs = gathered.at[q, pl.ds((1 - c) * NZ, NZ)]
            wait_bytes(theirs, ag_other.at[q])
            rows_even = gathered[q, :, 0:HALF, :].reshape(ROWS, CW)
            rows_odd = gathered[q, :, HALF:BLOCK, :].reshape(ROWS, CW)

            @pl.when(q < NF)
            def _():
                pre[...] += dot(rows_even, wide[cols_of(2 * q), :]) + dot(rows_odd, wide[cols_of(2 * q + 1), :])

            @pl.when(q >= NF)
            def _():
                k = q - NF
                down_copy(2 * k).wait()
                down_copy(2 * k + 1).wait()
                dhid[...] += dot_nt(rows_even, down[2 * k]) + dot_nt(rows_odd, down[2 * k + 1])

            pl.when(q == NF - 1)(activate)
            pl.when(q == NQ - 1)(activate_back)

        @pl.when((r >= 0) & (r < NQ))
        def _():
            q = r

            @pl.when(q >= 2)
            def _():
                wait_bytes(other.at[q - 2], ps.at[q - 2])

            def keep(parts):
                for j in range(2 * NZ):
                    for h in range(2):
                        base = (q % 2) * 2 * GROUP + j * BLOCK + h * HALF
                        partial[pl.ds(pl.multiple_of(base, PAD), HALF), :] = parts[h][j * HALF : (j + 1) * HALF]

            @pl.when(q < NF)
            def _():
                keep([dot(hid[...], down[2 * q + h]).astype(BF16) for h in range(2)])

            @pl.when(q >= NF)
            def _():
                keep([dot_nt(dpre[...], wide[cols_of(2 * (q - NF) + h), :]).astype(BF16) for h in range(2)])

            remote(partial.at[partial_rows(q, 1 - c, 0, GROUP)], other.at[q], ps.at[q], pr.at[q], partner)

        @pl.when((r >= 1) & (r < NQ + 1))
        def _():
            q = r - 1

            @pl.when(q >= 4)
            def _():
                wait_bytes(other.at[q - 4, pl.ds(0, GROUP - BLOCK)], ss.at[q - 4])

            wait_bytes(other.at[q], pr.at[q])
            sums[sum_rows(q, 0), :] = pair_sum(q, z_far, BLOCK, 0).astype(BF16)
            remote(sums.at[sum_rows(q, 0, HALF)], far_lo.at[q], ss.at[q], rr_far_lo.at[q], up)
            remote(sums.at[sum_rows(q, 0, HALF, HALF)], far_hi.at[q], ss.at[q], rr_far_hi.at[q], dn)
            sums[sum_rows(q, 1), :] = pair_sum(q, z_up, BLOCK, 0).astype(BF16)
            remote(sums.at[sum_rows(q, 1, HALF, HALF)], ring_lo.at[q, upper], ss.at[q], rr_lo.at[q], up)
            sums[sum_rows(q, 2), :] = pair_sum(q, z_dn, BLOCK, 0).astype(BF16)
            remote(sums.at[sum_rows(q, 2, HALF)], ring_hi.at[q, lower], ss.at[q], rr_hi.at[q], dn)
            sums[sum_rows(q, 3), :] = pair_sum(q, z, BLOCK, 0).astype(BF16)

        @pl.when((r >= 2) & (r < NQ + 2))
        def _():
            q = r - 2
            wait_bytes(far_lo.at[q], rr_far_lo.at[q])
            rows = sum_rows(q, 1, HALF)
            sums[rows, :] = (sums[rows, :].astype(F32) + far_lo[q].astype(F32)).astype(BF16)
            remote(sums.at[rows], ring_lo.at[q, lower], ss.at[q], rr_lo.at[q], up)
            wait_bytes(far_hi.at[q], rr_far_hi.at[q])
            rows = sum_rows(q, 2, HALF, HALF)
            sums[rows, :] = (sums[rows, :].astype(F32) + far_hi[q].astype(F32)).astype(BF16)
            remote(sums.at[rows], ring_hi.at[q, upper], ss.at[q], rr_hi.at[q], dn)

        @pl.when((r >= 3) & (r < NQ + 3))
        def _():
            q = r - 3
            wait_bytes(ring_lo.at[q], rr_lo.at[q])
            wait_bytes(ring_hi.at[q], rr_hi.at[q])
            wait_packet_sends(q, fs)
            wait_bytes(gathered.at[q, pl.ds(0, 7)], ags.at[q])

            total = (
                sums[sum_rows(q, 3), :].astype(F32) + ring_lo[q].astype(F32) + ring_hi[q].astype(F32)
            ).astype(BF16)
            rows = jnp.concatenate([total[0:HALF], total[HALF:BLOCK]], axis=1)
            pack[q] = dot(expand[...], segments(rows)).astype(BF16)
            send_packets(q, back_at, ts, tr.at[q])

        @pl.when((r >= 4) & (r < NQ + 4))
        def _():
            q = r - 4
            slot = q % 2

            @pl.when(q >= 2)
            def _():
                fin_copy(q - 2, mixed_hbm).wait()

            wait_bytes(back.at[q], tr.at[q])

            @pl.when(q >= 1)
            def _():
                wait_packet_sends(q - 1, ts)

            def result(rows):
                done = dot(finish[...], rows).astype(BF16)
                st_fin[slot, :, 0:SEG] = done[0:TOKENS]
                st_fin[slot, :, SEG : 2 * SEG] = done[TOKENS : 2 * TOKENS]
                st_fin[slot, :, 2 * SEG : PAIR] = done[2 * TOKENS :, 0 : PAIR - 2 * SEG]

            @pl.when(q < NF)
            def _():
                rows = back[q]
                result((rows.astype(F32) * row_scale[:, 0:1]).astype(BF16))
                fin_copy(q, mixed_hbm).start()
                part = (lax.broadcasted_iota(jnp.int32, (PACK, TOKENS), 0) % PAD) // CAP
                scores[...] += jnp.where(
                    part == 0,
                    dot_nt(rows, cot[q, :, 0:SEG]),
                    jnp.where(
                        part == 1,
                        dot_nt(rows, cot[q, :, SEG : 2 * SEG]),
                        dot_nt(rows[:, 0 : PAIR - 2 * SEG], cot[q, :, 2 * SEG : PAIR]),
                    ),
                )

            @pl.when(q >= NF)
            def _():
                result(back[q])
                fin_copy(q, dtok_hbm).start()

            @pl.when(q == NF)
            def _():
                by_slot = chosen[...] * scores[...]
                for k in range(TOP):
                    hit = ids_ref[k : k + 1, :] == lax.broadcasted_iota(jnp.int32, (PACK, TOKENS), 0) // PAD
                    dw_ref[k : k + 1, :] = jnp.sum(jnp.where(hit, by_slot, 0.0), axis=0, keepdims=True)
                dw_copy.start()

        for h in range(2):

            @pl.when((t >= GRADS) & (t < GRADS + NF))
            def _():
                g = t - GRADS
                q = 2 * g + h

                @pl.when(q >= 2)
                def _():
                    for copy in grad_copies(q - 2):
                        copy.wait()

                dec = gathered[g, :, h * HALF : (h + 1) * HALF, :].reshape(ROWS, CW)
                grd = gathered[NF + g, :, h * HALF : (h + 1) * HALF, :].reshape(ROWS, CW)
                st_down[h] = dot(hid_t[...], grd).astype(BF16)
                st_wide[h] = dot(dpre_t[...], dec).T.astype(BF16)
                for copy in grad_copies(q):
                    copy.start()

    for q in (NQ - 2, NQ - 1):
        wait_bytes(other.at[q], ps.at[q])
        for copy in grad_copies(q) + (fin_copy(q, dtok_hbm),):
            copy.wait()
    for q in range(NQ - 4, NQ):
        wait_bytes(other.at[q, pl.ds(0, GROUP - BLOCK)], ss.at[q])

    wait_packet_sends(NQ - 1, ts)
    dw_copy.wait()


def copy_out(*refs):
    count = (len(refs) - 2) // 3
    sources, results, held = refs[:count], refs[count : 2 * count], refs[2 * count : 3 * count]
    in_sem, out_sem = refs[3 * count :]
    reads, writes = [], []
    for i in range(count):
        rows = held[i].shape[0] // PARTS
        for p in range(PARTS if rows >= 16 else 1):
            part = pl.ds(p * rows, rows) if rows >= 16 else pl.ds(0, held[i].shape[0])
            reads.append(pltpu.make_async_copy(sources[i].at[part], held[i].at[part], in_sem.at[i, p]))
            writes.append(pltpu.make_async_copy(held[i].at[part], results[i].at[part], out_sem.at[i, p]))
    for copy in reads:
        copy.start()
    for read, write in zip(reads, writes):
        read.wait()
        write.start()
    for copy in writes:
        copy.wait()


def on_device(tokens, expert_ids, route_weights, grad_out, gate_weight, up_weight, down_weight):
    any_spec = pl.BlockSpec(memory_space=pl.ANY)
    shape = jax.ShapeDtypeStruct
    dma = pltpu.SemaphoreType.DMA
    outs = (
        shape((TOKENS, D), BF16),
        shape((TOKENS, D), BF16),
        shape((TOP, TOKENS), F32),
        shape((D, HID), BF16),
        shape((D, HID), BF16),
        shape((HID, D), BF16),
    )
    results = pl.pallas_call(
        kernel,
        out_shape=outs,
        in_specs=[any_spec] * 7,
        out_specs=(any_spec,) * 6,
        scratch_shapes=[
            pltpu.VMEM((NQ, PACK, SEG), BF16),
            pltpu.VMEM((NQ, PACK, SEG), BF16),
            pltpu.VMEM((4 * GROUP, CW), BF16),
            pltpu.VMEM((NQ, 2 * NZ, BLOCK, CW), BF16),
            pltpu.VMEM((D, 2 * HID), BF16),
            pltpu.VMEM((NQ, HID, CW), BF16),
            pltpu.VMEM((NF, TOKENS, PAIR), BF16),
            pltpu.VMEM((4 * GROUP, CW), BF16),
            pltpu.VMEM((NQ, GROUP, CW), BF16),
            pltpu.VMEM((NQ, BLOCK, CW), BF16),
            pltpu.VMEM((NQ, BLOCK, CW), BF16),
            pltpu.VMEM((NQ, HALF, CW), BF16),
            pltpu.VMEM((NQ, HALF, CW), BF16),
            pltpu.VMEM((NQ, PACK, SEG), BF16),
            pltpu.VMEM((2, TOKENS, PAIR), BF16),
            pltpu.VMEM((2, HID, CW), BF16),
            pltpu.VMEM((2, CW, 2 * HID), BF16),
            pltpu.VMEM((TOP, TOKENS), jnp.int32),
            pltpu.VMEM((TOP, TOKENS), F32),
            pltpu.VMEM((TOP, TOKENS), F32),
            pltpu.VMEM((PACK, TOKENS), F32),
            pltpu.VMEM((PACK, SEGS * TOKENS), BF16),
            pltpu.VMEM((SEGS * TOKENS, PACK), BF16),
            pltpu.VMEM((SEGS * HALF, PACK), BF16),
            pltpu.VMEM((PACK, SEGS * HALF), BF16),
            pltpu.VMEM((PACK, 128), F32),
            pltpu.VMEM((ROWS, 2 * HID), F32),
            pltpu.VMEM((ROWS, HID), F32),
            pltpu.VMEM((ROWS, HID), BF16),
            pltpu.VMEM((ROWS, 2 * HID), BF16),
            pltpu.VMEM((HID, ROWS), BF16),
            pltpu.VMEM((2 * HID, ROWS), BF16),
            pltpu.VMEM((PACK, TOKENS), F32),
            dma((4, NQ)),
        ]
        + [dma((NQ,))] * 17
        + [dma((2,)), dma((3, 2))],
        compiler_params=pltpu.CompilerParams(
            collective_id=0, has_side_effects=True, vmem_limit_bytes=VMEM_LIMIT
        ),
        cost_estimate=pl.CostEstimate(
            flops=9 * 2 * ROWS * D * HID, bytes_accessed=10 * D * 256, transcendentals=ROWS * HID
        ),
        name="expert_layer",
    )(expert_ids.T, route_weights.T, tokens, grad_out, gate_weight, up_weight, down_weight)
    mixed, dtok, dw, dgate, dup, ddown = pl.pallas_call(
        copy_out,
        out_shape=outs,
        in_specs=[any_spec] * 6,
        out_specs=(any_spec,) * 6,
        scratch_shapes=[pltpu.VMEM(o.shape, o.dtype) for o in outs] + [dma((6, PARTS)), dma((6, PARTS))],
        compiler_params=pltpu.CompilerParams(vmem_limit_bytes=VMEM_LIMIT),
        name="copy_out",
    )(*results)
    return (mixed, dtok, dw.T, dgate, dup, ddown)


def solution(mesh):
    rows = P(("node", "local"), None)
    cols = P(None, ("node", "local"))
    return jax.shard_map(
        on_device,
        mesh=mesh,
        in_specs=(rows, rows, rows, rows, cols, cols, rows),
        out_specs=(rows, rows, rows, cols, cols, rows),
        check_vma=False,
    )
```

```python
import functools

import jax
import jax.numpy as jnp
from jax import lax
from jax.experimental import pallas as pl
from jax.experimental.pallas import tpu as pltpu
from jax.sharding import PartitionSpec as P

F32 = jnp.float32
BF16 = jnp.bfloat16
MESH = pl.DeviceIdType.MESH

TOKENS = 128
TOP = 8
D = 7168
HID = 128
NX, NY, NZ = 4, 4, 4
EXPERTS = NX * NY
CAP = 5
PAD = 16
SEGS = 3
PACK = EXPERTS * PAD
HALF = EXPERTS * CAP
BLOCK = 2 * HALF
GROUP = NZ * BLOCK
ROWS = 2 * NZ * HALF
CW = 512
NQ = D // CW
NF = NQ // 2
AHEAD = 2
PAIR = 2 * CW
SEG = 384
BACK = 12
GRADS = NQ + 3
PARTS = 4
VMEM_LIMIT = 64 * 1024 * 1024 - 1024 * 1024


def dot(a, b):
    return jnp.dot(a, b, preferred_element_type=F32)


def dot_nt(a, b):
    return lax.dot_general(a, b, (((1,), (1,)), ((), ())), preferred_element_type=F32)


def kernel(
    ids_hbm,
    weights_hbm,
    tokens_hbm,
    cot_hbm,
    gate_hbm,
    up_hbm,
    down_hbm,
    mixed_hbm,
    dtok_hbm,
    dw_hbm,
    dgate_hbm,
    dup_hbm,
    ddown_hbm,
    pack,
    inbox,
    partial,
    gathered,
    wide,
    down,
    cot,
    sums,
    other,
    ring_lo,
    ring_hi,
    far_lo,
    far_hi,
    back,
    st_fin,
    st_down,
    st_wide,
    ids_ref,
    weights_ref,
    dw_ref,
    chosen,
    select,
    finish,
    compact,
    expand,
    row_scale,
    pre,
    dhid,
    hid,
    dpre,
    hid_t,
    dpre_t,
    scores,
    load_sem,
    fs,
    fr,
    ags,
    ag_other,
    ag_lo,
    ag_hi,
    ag_far_lo,
    ag_far_hi,
    ps,
    pr,
    ss,
    rr_lo,
    rr_hi,
    rr_far_lo,
    rr_far_hi,
    ts,
    tr,
    fin_sem,
    grad_sem,
):
    x = lax.axis_index("node")
    local = lax.axis_index("local")
    y = local // (2 * NZ)
    z = (local // 2) % NZ
    c = local % 2
    z_up, z_dn, z_far = (z + 1) % NZ, (z + NZ - 1) % NZ, (z + 2) % NZ
    here = x * NY + y
    me = c * NZ + z
    partner = (x, y * 2 * NZ + z * 2 + (1 - c))
    up = (x, y * 2 * NZ + z_up * 2 + c)
    dn = (x, y * 2 * NZ + z_dn * 2 + c)

    def peer(k):
        px = (x + k // NY) % NX
        py = (y + k % NY) % NY
        return px * NY + py, (px, py * 2 * NZ + z * 2 + c)

    def cols_of(q):
        return pl.ds(pl.multiple_of(q * CW, CW), CW)

    def pair_of(q):
        return pl.ds(pl.multiple_of(q * PAIR, PAIR), PAIR)

    def token_rows(q):
        return pl.ds(pl.multiple_of(q * TOKENS, TOKENS), TOKENS)

    def token_copy(q):
        return pltpu.make_async_copy(tokens_hbm.at[:, cols_of(q)], sums.at[token_rows(q)], load_sem.at[0, q])

    def cot_copy(q):
        return pltpu.make_async_copy(cot_hbm.at[:, pair_of(q)], cot.at[q], load_sem.at[1, q])

    def down_copy(q):
        return pltpu.make_async_copy(down_hbm.at[:, cols_of(q)], down.at[q], load_sem.at[2, q])

    ids_copy = pltpu.make_async_copy(ids_hbm, ids_ref, load_sem.at[3, 0])
    weights_copy = pltpu.make_async_copy(weights_hbm, weights_ref, load_sem.at[3, 1])
    gate_copy = pltpu.make_async_copy(gate_hbm, wide.at[:, pl.ds(0, HID)], load_sem.at[3, 2])
    up_copy = pltpu.make_async_copy(up_hbm, wide.at[:, pl.ds(HID, HID)], load_sem.at[3, 3])
    ids_copy.start()
    weights_copy.start()

    @pl.loop(0, NQ)
    def _(q):
        token_copy(q).start()

    gate_copy.start()
    up_copy.start()

    @pl.loop(0, NF)
    def _(q):
        cot_copy(q).start()
        down_copy(2 * q).start()
        down_copy(2 * q + 1).start()

    barrier = pltpu.get_barrier_semaphore()

    @pl.loop(1, EXPERTS)
    def _(k):
        _, device = peer(k)
        pl.semaphore_signal(barrier, inc=1, device_id=device, device_id_type=MESH)

    for device in (partner, up, dn):
        pl.semaphore_signal(barrier, inc=1, device_id=device, device_id_type=MESH)

    ids_copy.wait()
    weights_copy.wait()
    row = lax.broadcasted_iota(jnp.int32, (PACK, TOKENS), 0)
    expert, place = row // PAD, row % PAD
    segment = place // CAP
    rank_of = jnp.where(segment < SEGS, place % CAP, -1).astype(F32)
    named = jnp.zeros((PACK, TOKENS), F32)
    weight_of = jnp.zeros((PACK, TOKENS), F32)
    for k in range(TOP):
        hit = ids_ref[k : k + 1, :] == expert
        named = jnp.where(hit, 1.0, named)
        weight_of = jnp.where(hit, weights_ref[k : k + 1, :], weight_of)
    earlier = lax.broadcasted_iota(jnp.int32, (TOKENS, TOKENS), 0) < lax.broadcasted_iota(
        jnp.int32, (TOKENS, TOKENS), 1
    )
    rank = dot(named.astype(BF16), jnp.where(earlier, 1.0, 0.0).astype(BF16))
    picks = jnp.where((named > 0.5) & (rank == rank_of), 1.0, 0.0)
    chosen[...] = picks
    for k in range(SEGS):
        select[:, pl.ds(k * TOKENS, TOKENS)] = jnp.where(segment == k, picks, 0.0).astype(BF16)
    row_scale[...] = jnp.broadcast_to(jnp.sum(picks * weight_of, axis=1, keepdims=True), (PACK, 128))

    def slot_target(shape, dim):
        r = lax.broadcasted_iota(jnp.int32, shape, dim)
        e, i = r // PAD, r % PAD
        return jnp.where(i < SEGS * CAP, (i // CAP) * HALF + e * CAP + i % CAP, -1)

    def send_packets(q, dst_at, send_sem, recv_sem):
        pltpu.make_async_copy(
            pack.at[q, pl.ds(pl.multiple_of(here * PAD, PAD), PAD)], dst_at(q, here), recv_sem
        ).start()

        @pl.loop(1, EXPERTS)
        def _(k):
            e, device = peer(k)
            pltpu.make_async_remote_copy(
                src_ref=pack.at[q, pl.ds(pl.multiple_of(e * PAD, PAD), PAD)],
                dst_ref=dst_at(q, here),
                send_sem=send_sem.at[q],
                recv_sem=recv_sem,
                device_id=device,
                device_id_type=MESH,
            ).start()

    def inbox_at(q, e):
        return inbox.at[q, pl.ds(pl.multiple_of(e * PAD, PAD), PAD)]

    def back_at(q, e):
        return back.at[q, pl.ds(pl.multiple_of(e * PAD, PAD), PAD)]

    def wait_bytes(ref, sem):
        pltpu.make_async_copy(ref, ref, sem).wait()

    def wait_packet_sends(q, send_sem):
        wait_bytes(pack.at[q, pl.ds(0, PACK - PAD)], send_sem.at[q])

    def decode(q):
        token_copy(q).wait()
        values = sums[token_rows(q), :].astype(F32)
        parts = []
        for b in range(CW // 128):
            v = values[:, b * 128 : (b + 1) * 128]
            scale = (jnp.max(jnp.abs(v), axis=1, keepdims=True) + 1e-06).astype(BF16).astype(F32)
            code = (v / scale).astype(BF16).astype(F32)
            parts.append((code * scale).astype(BF16))
        return parts

    def segments(rows):
        short = rows[:, 2 * SEG :]
        zeros = jnp.zeros((rows.shape[0], SEGS * SEG - PAIR), BF16)
        return jnp.concatenate([rows[:, :SEG], rows[:, SEG : 2 * SEG], jnp.concatenate([short, zeros], axis=1)], axis=0)

    def prepare(q):
        @pl.when(q < NF)
        def _():
            decoded = jnp.concatenate(decode(2 * q) + decode(2 * q + 1), axis=1)
            pack[q] = dot(select[...], segments(decoded)).astype(BF16)

        @pl.when(q >= NF)
        def _():
            cot_copy(q - NF).wait()
            pack[q] = (dot(select[...], segments(cot[q - NF])) * row_scale[:, 0:1]).astype(BF16)

    def send_forward(q):
        send_packets(q, inbox_at, fs, fr.at[q])

    def remote(src, dst, send_sem, recv_sem, device):
        pltpu.make_async_remote_copy(
            src_ref=src, dst_ref=dst, send_sem=send_sem, recv_sem=recv_sem, device_id=device, device_id_type=MESH
        ).start()

    lower, upper = pl.ds(0, HALF), pl.ds(HALF, HALF)

    def activate():
        @pl.loop(0, ROWS // HID)
        def _(i):
            rows = pl.ds(pl.multiple_of(i * HID, HID), HID)
            gate_pre = pre[rows, 0:HID]
            sig = 1.0 / (1.0 + jnp.exp(-gate_pre))
            hid[rows, :] = (gate_pre * sig * pre[rows, HID : 2 * HID]).astype(BF16)

        for i in range(ROWS // HID):
            rows = slice(i * HID, (i + 1) * HID)
            hid_t[:, rows] = hid[rows, :].astype(F32).T.astype(BF16)

    def activate_back():
        @pl.loop(0, ROWS // HID)
        def _(i):
            rows = pl.ds(pl.multiple_of(i * HID, HID), HID)
            gate_pre = pre[rows, 0:HID]
            grad_hidden = dhid[rows, :]
            sig = 1.0 / (1.0 + jnp.exp(-gate_pre))
            slope = sig * (1.0 + gate_pre * (1.0 - sig))
            dpre[rows, 0:HID] = (grad_hidden * pre[rows, HID : 2 * HID] * slope).astype(BF16)
            dpre[rows, HID : 2 * HID] = (grad_hidden * (gate_pre * sig)).astype(BF16)

        for i in range(ROWS // HID):
            rows = slice(i * HID, (i + 1) * HID)
            dpre_t[0:HID, rows] = dpre[rows, 0:HID].astype(F32).T.astype(BF16)
            dpre_t[HID : 2 * HID, rows] = dpre[rows, HID : 2 * HID].astype(F32).T.astype(BF16)

    def partial_rows(q, side, zz, size=BLOCK, offset=0):
        start = (q % 2) * 2 * GROUP + side * GROUP + zz * BLOCK + offset
        return pl.ds(pl.multiple_of(start, PAD), size)

    def other_rows(zz, size=BLOCK, offset=0):
        return pl.ds(pl.multiple_of(zz * BLOCK + offset, PAD), size)

    def sum_rows(q, k, size=BLOCK, offset=0):
        return pl.ds(pl.multiple_of((q % 4) * GROUP + k * BLOCK + offset, PAD), size)

    def grad_copies(q):
        slot = q % 2
        rows = cols_of(q)
        return (
            pltpu.make_async_copy(st_down.at[slot], ddown_hbm.at[:, rows], grad_sem.at[0, slot]),
            pltpu.make_async_copy(st_wide.at[slot, :, pl.ds(0, HID)], dgate_hbm.at[rows], grad_sem.at[1, slot]),
            pltpu.make_async_copy(st_wide.at[slot, :, pl.ds(HID, HID)], dup_hbm.at[rows], grad_sem.at[2, slot]),
        )

    def fin_copy(q, out_hbm):
        slot = q % 2
        return pltpu.make_async_copy(st_fin.at[slot], out_hbm.at[:, pair_of(q % NF)], fin_sem.at[slot])

    def pair_sum(q, zz, size, offset):
        mine = partial[partial_rows(q, c, zz, size, offset), :].astype(F32)
        return mine + other[q, other_rows(zz, size, offset), :].astype(F32)

    dw_copy = pltpu.make_async_copy(dw_ref, dw_hbm, load_sem.at[3, 0])

    def keep_own(q):
        wait_bytes(inbox.at[q], fr.at[q])
        kept = dot(compact[...], inbox[q]).astype(BF16)
        gathered[q, me, 0:HALF, 0:SEG] = kept[0:HALF]
        gathered[q, me, 0:HALF, SEG:CW] = kept[HALF : 2 * HALF, 0 : CW - SEG]
        gathered[q, me, HALF:BLOCK, 0 : 2 * SEG - CW] = kept[HALF : 2 * HALF, CW - SEG : SEG]
        gathered[q, me, HALF:BLOCK, 2 * SEG - CW : CW] = kept[2 * HALF :, 0 : PAIR - 2 * SEG]
        mine = gathered.at[q, me]
        remote(mine, mine, ags.at[q], ag_lo.at[q], up)
        remote(mine, mine, ags.at[q], ag_hi.at[q], dn)
        remote(mine, mine, ags.at[q], ag_other.at[q], partner)

    prepare(0)
    pl.semaphore_wait(barrier, EXPERTS - 1 + 3)
    send_forward(0)
    compact[...] = jnp.where(
        lax.broadcasted_iota(jnp.int32, (SEGS * HALF, PACK), 0) == slot_target((SEGS * HALF, PACK), 1), 1.0, 0.0
    ).astype(BF16)
    prepare(1)
    send_forward(1)
    keep_own(0)
    prepare(2)
    send_forward(2)
    for k in range(SEGS):
        finish[pl.ds(k * TOKENS, TOKENS), :] = jnp.where(segment == k, chosen[...], 0.0).T.astype(BF16)
    expand[...] = jnp.where(
        lax.broadcasted_iota(jnp.int32, (PACK, SEGS * HALF), 1) == slot_target((PACK, SEGS * HALF), 0), 1.0, 0.0
    ).astype(BF16)
    pre[...] = jnp.zeros_like(pre)
    dhid[...] = jnp.zeros_like(dhid)
    scores[...] = jnp.zeros_like(scores)

    @pl.loop(1, BACK + NQ + 4)
    def _(t):
        r = t - BACK

        @pl.when(t < NQ)
        def _():
            keep_own(t)

        @pl.when((t >= 1) & (t < NQ + 1))
        def _():
            q = t - 1
            from_lo = gathered.at[q, c * NZ + z_dn]
            wait_bytes(from_lo, ag_lo.at[q])
            half = gathered.at[q, c * NZ + z_dn, lower]
            remote(half, half, ags.at[q], ag_far_lo.at[q], up)
            remote(from_lo, from_lo, ags.at[q], ag_other.at[q], partner)
            from_hi = gathered.at[q, c * NZ + z_up]
            wait_bytes(from_hi, ag_hi.at[q])
            half = gathered.at[q, c * NZ + z_up, upper]
            remote(half, half, ags.at[q], ag_far_hi.at[q], dn)
            remote(from_hi, from_hi, ags.at[q], ag_other.at[q], partner)

        @pl.when(t + AHEAD < NQ)
        def _():
            prepare(t + AHEAD)
            send_forward(t + AHEAD)

        @pl.when((t >= 2) & (t < NQ + 2))
        def _():
            q = t - 2
            half = gathered.at[q, c * NZ + z_far, lower]
            wait_bytes(half, ag_far_lo.at[q])
            remote(half, half, ags.at[q], ag_other.at[q], partner)
            half = gathered.at[q, c * NZ + z_far, upper]
            wait_bytes(half, ag_far_hi.at[q])
            remote(half, half, ags.at[q], ag_other.at[q], partner)

        @pl.when(t == 3)
        def _():
            gate_copy.wait()
            up_copy.wait()

        @pl.when((t >= 3) & (t < NQ + 3))
        def _():
            q = t - 3
            theirs = gathered.at[q, pl.ds((1 - c) * NZ, NZ)]
            wait_bytes(theirs, ag_other.at[q])
            rows_even = gathered[q, :, 0:HALF, :].reshape(ROWS, CW)
            rows_odd = gathered[q, :, HALF:BLOCK, :].reshape(ROWS, CW)

            @pl.when(q < NF)
            def _():
                pre[...] += dot(rows_even, wide[cols_of(2 * q), :]) + dot(rows_odd, wide[cols_of(2 * q + 1), :])

            @pl.when(q >= NF)
            def _():
                k = q - NF
                down_copy(2 * k).wait()
                down_copy(2 * k + 1).wait()
                dhid[...] += dot_nt(rows_even, down[2 * k]) + dot_nt(rows_odd, down[2 * k + 1])

            pl.when(q == NF - 1)(activate)
            pl.when(q == NQ - 1)(activate_back)

        @pl.when((r >= 0) & (r < NQ))
        def _():
            q = r

            @pl.when(q >= 2)
            def _():
                wait_bytes(other.at[q - 2], ps.at[q - 2])

            def keep(parts):
                for j in range(2 * NZ):
                    for h in range(2):
                        base = (q % 2) * 2 * GROUP + j * BLOCK + h * HALF
                        partial[pl.ds(pl.multiple_of(base, PAD), HALF), :] = parts[h][j * HALF : (j + 1) * HALF]

            @pl.when(q < NF)
            def _():
                keep([dot(hid[...], down[2 * q + h]).astype(BF16) for h in range(2)])

            @pl.when(q >= NF)
            def _():
                keep([dot_nt(dpre[...], wide[cols_of(2 * (q - NF) + h), :]).astype(BF16) for h in range(2)])

            remote(partial.at[partial_rows(q, 1 - c, 0, GROUP)], other.at[q], ps.at[q], pr.at[q], partner)

        @pl.when((r >= 2) & (r < NQ + 2))
        def _():
            q = r - 2
            wait_bytes(far_lo.at[q], rr_far_lo.at[q])
            rows = sum_rows(q, 1, HALF)
            sums[rows, :] = (sums[rows, :].astype(F32) + far_lo[q].astype(F32)).astype(BF16)
            remote(sums.at[rows], ring_lo.at[q, lower], ss.at[q], rr_lo.at[q], up)
            wait_bytes(far_hi.at[q], rr_far_hi.at[q])
            rows = sum_rows(q, 2, HALF, HALF)
            sums[rows, :] = (sums[rows, :].astype(F32) + far_hi[q].astype(F32)).astype(BF16)
            remote(sums.at[rows], ring_hi.at[q, upper], ss.at[q], rr_hi.at[q], dn)

        @pl.when((r >= 1) & (r < NQ + 1))
        def _():
            q = r - 1

            @pl.when(q >= 4)
            def _():
                wait_bytes(other.at[q - 4, pl.ds(0, GROUP - BLOCK)], ss.at[q - 4])

            wait_bytes(other.at[q], pr.at[q])
            sums[sum_rows(q, 0), :] = pair_sum(q, z_far, BLOCK, 0).astype(BF16)
            remote(sums.at[sum_rows(q, 0, HALF)], far_lo.at[q], ss.at[q], rr_far_lo.at[q], up)
            remote(sums.at[sum_rows(q, 0, HALF, HALF)], far_hi.at[q], ss.at[q], rr_far_hi.at[q], dn)
            sums[sum_rows(q, 1), :] = pair_sum(q, z_up, BLOCK, 0).astype(BF16)
            remote(sums.at[sum_rows(q, 1, HALF, HALF)], ring_lo.at[q, upper], ss.at[q], rr_lo.at[q], up)
            sums[sum_rows(q, 2), :] = pair_sum(q, z_dn, BLOCK, 0).astype(BF16)
            remote(sums.at[sum_rows(q, 2, HALF)], ring_hi.at[q, lower], ss.at[q], rr_hi.at[q], dn)
            sums[sum_rows(q, 3), :] = pair_sum(q, z, BLOCK, 0).astype(BF16)

        @pl.when((r >= 3) & (r < NQ + 3))
        def _():
            q = r - 3
            wait_bytes(ring_lo.at[q], rr_lo.at[q])
            wait_bytes(ring_hi.at[q], rr_hi.at[q])
            wait_packet_sends(q, fs)
            wait_bytes(gathered.at[q, pl.ds(0, 7)], ags.at[q])

            total = (
                sums[sum_rows(q, 3), :].astype(F32) + ring_lo[q].astype(F32) + ring_hi[q].astype(F32)
            ).astype(BF16)
            rows = jnp.concatenate([total[0:HALF], total[HALF:BLOCK]], axis=1)
            pack[q] = dot(expand[...], segments(rows)).astype(BF16)
            send_packets(q, back_at, ts, tr.at[q])

        @pl.when((r >= 4) & (r < NQ + 4))
        def _():
            q = r - 4
            slot = q % 2

            @pl.when(q >= 2)
            def _():
                fin_copy(q - 2, mixed_hbm).wait()

            wait_bytes(back.at[q], tr.at[q])

            @pl.when(q >= 1)
            def _():
                wait_packet_sends(q - 1, ts)

            def result(rows):
                done = dot(finish[...], rows).astype(BF16)
                st_fin[slot, :, 0:SEG] = done[0:TOKENS]
                st_fin[slot, :, SEG : 2 * SEG] = done[TOKENS : 2 * TOKENS]
                st_fin[slot, :, 2 * SEG : PAIR] = done[2 * TOKENS :, 0 : PAIR - 2 * SEG]

            @pl.when(q < NF)
            def _():
                rows = back[q]
                result((rows.astype(F32) * row_scale[:, 0:1]).astype(BF16))
                fin_copy(q, mixed_hbm).start()
                part = (lax.broadcasted_iota(jnp.int32, (PACK, TOKENS), 0) % PAD) // CAP
                scores[...] += jnp.where(
                    part == 0,
                    dot_nt(rows, cot[q, :, 0:SEG]),
                    jnp.where(
                        part == 1,
                        dot_nt(rows, cot[q, :, SEG : 2 * SEG]),
                        dot_nt(rows[:, 0 : PAIR - 2 * SEG], cot[q, :, 2 * SEG : PAIR]),
                    ),
                )

            @pl.when(q >= NF)
            def _():
                result(back[q])
                fin_copy(q, dtok_hbm).start()

            @pl.when(q == NF)
            def _():
                by_slot = chosen[...] * scores[...]
                for k in range(TOP):
                    hit = ids_ref[k : k + 1, :] == lax.broadcasted_iota(jnp.int32, (PACK, TOKENS), 0) // PAD
                    dw_ref[k : k + 1, :] = jnp.sum(jnp.where(hit, by_slot, 0.0), axis=0, keepdims=True)
                dw_copy.start()

        for h in range(2):

            @pl.when((t >= GRADS) & (t < GRADS + NF))
            def _():
                g = t - GRADS
                q = 2 * g + h

                @pl.when(q >= 2)
                def _():
                    for copy in grad_copies(q - 2):
                        copy.wait()

                dec = gathered[g, :, h * HALF : (h + 1) * HALF, :].reshape(ROWS, CW)
                grd = gathered[NF + g, :, h * HALF : (h + 1) * HALF, :].reshape(ROWS, CW)
                st_down[h] = dot(hid_t[...], grd).astype(BF16)
                st_wide[h] = dot(dpre_t[...], dec).T.astype(BF16)
                for copy in grad_copies(q):
                    copy.start()

    for q in (NQ - 2, NQ - 1):
        wait_bytes(other.at[q], ps.at[q])
        for copy in grad_copies(q) + (fin_copy(q, dtok_hbm),):
            copy.wait()
    for q in range(NQ - 4, NQ):
        wait_bytes(other.at[q, pl.ds(0, GROUP - BLOCK)], ss.at[q])

    wait_packet_sends(NQ - 1, ts)
    dw_copy.wait()


def copy_out(*refs):
    count = (len(refs) - 2) // 3
    sources, results, held = refs[:count], refs[count : 2 * count], refs[2 * count : 3 * count]
    in_sem, out_sem = refs[3 * count :]
    reads, writes = [], []
    for i in range(count):
        rows = held[i].shape[0] // PARTS
        for p in range(PARTS if rows >= 16 else 1):
            part = pl.ds(p * rows, rows) if rows >= 16 else pl.ds(0, held[i].shape[0])
            reads.append(pltpu.make_async_copy(sources[i].at[part], held[i].at[part], in_sem.at[i, p]))
            writes.append(pltpu.make_async_copy(held[i].at[part], results[i].at[part], out_sem.at[i, p]))
    for copy in reads:
        copy.start()
    for read, write in zip(reads, writes):
        read.wait()
        write.start()
    for copy in writes:
        copy.wait()


def on_device(tokens, expert_ids, route_weights, grad_out, gate_weight, up_weight, down_weight):
    any_spec = pl.BlockSpec(memory_space=pl.ANY)
    shape = jax.ShapeDtypeStruct
    dma = pltpu.SemaphoreType.DMA
    outs = (
        shape((TOKENS, D), BF16),
        shape((TOKENS, D), BF16),
        shape((TOP, TOKENS), F32),
        shape((D, HID), BF16),
        shape((D, HID), BF16),
        shape((HID, D), BF16),
    )
    results = pl.pallas_call(
        kernel,
        out_shape=outs,
        in_specs=[any_spec] * 7,
        out_specs=(any_spec,) * 6,
        scratch_shapes=[
            pltpu.VMEM((NQ, PACK, SEG), BF16),
            pltpu.VMEM((NQ, PACK, SEG), BF16),
            pltpu.VMEM((4 * GROUP, CW), BF16),
            pltpu.VMEM((NQ, 2 * NZ, BLOCK, CW), BF16),
            pltpu.VMEM((D, 2 * HID), BF16),
            pltpu.VMEM((NQ, HID, CW), BF16),
            pltpu.VMEM((NF, TOKENS, PAIR), BF16),
            pltpu.VMEM((4 * GROUP, CW), BF16),
            pltpu.VMEM((NQ, GROUP, CW), BF16),
            pltpu.VMEM((NQ, BLOCK, CW), BF16),
            pltpu.VMEM((NQ, BLOCK, CW), BF16),
            pltpu.VMEM((NQ, HALF, CW), BF16),
            pltpu.VMEM((NQ, HALF, CW), BF16),
            pltpu.VMEM((NQ, PACK, SEG), BF16),
            pltpu.VMEM((2, TOKENS, PAIR), BF16),
            pltpu.VMEM((2, HID, CW), BF16),
            pltpu.VMEM((2, CW, 2 * HID), BF16),
            pltpu.VMEM((TOP, TOKENS), jnp.int32),
            pltpu.VMEM((TOP, TOKENS), F32),
            pltpu.VMEM((TOP, TOKENS), F32),
            pltpu.VMEM((PACK, TOKENS), F32),
            pltpu.VMEM((PACK, SEGS * TOKENS), BF16),
            pltpu.VMEM((SEGS * TOKENS, PACK), BF16),
            pltpu.VMEM((SEGS * HALF, PACK), BF16),
            pltpu.VMEM((PACK, SEGS * HALF), BF16),
            pltpu.VMEM((PACK, 128), F32),
            pltpu.VMEM((ROWS, 2 * HID), F32),
            pltpu.VMEM((ROWS, HID), F32),
            pltpu.VMEM((ROWS, HID), BF16),
            pltpu.VMEM((ROWS, 2 * HID), BF16),
            pltpu.VMEM((HID, ROWS), BF16),
            pltpu.VMEM((2 * HID, ROWS), BF16),
            pltpu.VMEM((PACK, TOKENS), F32),
            dma((4, NQ)),
        ]
        + [dma((NQ,))] * 17
        + [dma((2,)), dma((3, 2))],
        compiler_params=pltpu.CompilerParams(
            collective_id=0, has_side_effects=True, vmem_limit_bytes=VMEM_LIMIT
        ),
        cost_estimate=pl.CostEstimate(
            flops=9 * 2 * ROWS * D * HID, bytes_accessed=10 * D * 256, transcendentals=ROWS * HID
        ),
        name="expert_layer",
    )(expert_ids.T, route_weights.T, tokens, grad_out, gate_weight, up_weight, down_weight)
    mixed, dtok, dw, dgate, dup, ddown = pl.pallas_call(
        copy_out,
        out_shape=outs,
        in_specs=[any_spec] * 6,
        out_specs=(any_spec,) * 6,
        scratch_shapes=[pltpu.VMEM(o.shape, o.dtype) for o in outs] + [dma((6, PARTS)), dma((6, PARTS))],
        compiler_params=pltpu.CompilerParams(vmem_limit_bytes=VMEM_LIMIT),
        name="copy_out",
    )(*results)
    return (mixed, dtok, dw.T, dgate, dup, ddown)


def solution(mesh):
    rows = P(("node", "local"), None)
    cols = P(None, ("node", "local"))
    return jax.shard_map(
        on_device,
        mesh=mesh,
        in_specs=(rows, rows, rows, rows, cols, cols, rows),
        out_specs=(rows, rows, rows, cols, cols, rows),
        check_vma=False,
    )
```
